768 devices in a mesh: space: 64 (over x, y, core), segment: 12 (over z).
Axes of the slice: x: 4, y: 8, z: 12, core: 2. Of those that a mesh axis runs over, the one named last changes fastest.
Arguments:
- incoming: bfloat16 [12, 1024, 64, 128], P('segment', 'space'), may hold values from -6 to 6
- saved: bfloat16 [12, 1024, 64, 128], P('segment', 'space'), may hold values from -6 to 6
- cotangent: bfloat16 [12, 1024, 64, 128], P('segment', 'space'), may hold values from -6 to 6
- occupancy: int32 [12, 1024, 64], P('segment', 'space'), may hold values from 0 to 1, as said below
- neighbours: int32 [12, 1024, 27], P('segment', 'space'), may hold values from -1 to 1023, as said below
- conv_weight: bfloat16 [12, 27, 128, 128], P('segment'), may hold values from -0.15625 to 0.15625
Outputs:
- arrived: bfloat16 [12, 1024, 64, 128], P('segment', 'space')
- returned: bfloat16 [12, 1024, 64, 128], P('segment', 'space')
The draws below stay inside these ranges and needn't reach their ends.
Inputs may be any that keep to these rules, and one draw needn't show every extreme that they name: `neighbours`: per section: entry o = 9 (ex + 1) + 3 (ey + 1) + (ez + 1) of brick b names the brick at brick offset (ex, ey, ez) from b, or -1 where there is none. A named brick's number differs from b by at most 7. The relation is symmetric: b names c at o exactly when c names b at 26 - o. A present brick names itself at entry 13; a brick slot that is not present has all entries -1, no occupied voxel, and is named by no brick. `occupancy`: voxel u = 16 x + 4 y + z of a brick.
All inputs are finite; a program needn't handle non-finite values.
Results may differ from the reference program's by a relative error of at most 0.0034.
Values may be sent and summed in bfloat16 or wider, within the bound.
No kernel may reach another device: no remote copies, remote signals or barrier semaphores. Data moves between devices by JAX's collectives and lax.ppermute only.
A program may use at most 128 MiB of HBM per device.

```python
import jax
import jax.numpy as jnp
from jax import lax

C = 128
VOX = 64
BRICKS_DEV = 16
NBRICK = 1024
SEGMENTS = 12


def brick_layout(key):
    level_key, roll_key = jax.random.split(key)
    device_count = NBRICK // BRICKS_DEV
    levels = jax.random.randint(level_key, (SEGMENTS, device_count, 1), 3, 9)
    rolled = jax.random.randint(roll_key, (SEGMENTS, device_count, BRICKS_DEV), 0, 8)
    present = (rolled < levels).reshape(SEGMENTS, NBRICK)
    brick_ids = jnp.arange(NBRICK)
    edge_bricks = (brick_ids == 0) | (brick_ids == NBRICK - 1)
    return present | edge_bricks[None, :]


def draw_occupancy(key, part):
    present = brick_layout(key)
    key = jax.random.fold_in(key, 11)
    voxel_rolls = jax.random.randint(key, (SEGMENTS, NBRICK, VOX), 0, 8)
    filled = (voxel_rolls < 5) & present[:, :, None]
    return filled.astype(jnp.int32)


def draw_neighbours(key, part):
    present = brick_layout(key)
    brick_ids = jnp.arange(NBRICK)
    offsets = jnp.arange(27)
    step_x = offsets // 9 - 1
    step_y = offsets // 3 % 3 - 1
    step_z = offsets % 3 - 1
    target_x = (brick_ids // 4)[:, None] + step_x[None, :]
    target_y = (brick_ids // 2 % 2)[:, None] + step_y[None, :]
    target_z = (brick_ids % 2)[:, None] + step_z[None, :]
    inside = (target_x >= 0) & (target_x < NBRICK // 4) & (target_y >= 0) & (target_y < 2) & (target_z >= 0) & (target_z < 2)
    target = jnp.clip(target_x * 4 + target_y * 2 + target_z, 0, NBRICK - 1)
    target_present = present[:, target]
    valid = inside[None, :, :] & target_present & present[:, :, None]
    return jnp.where(valid, target[None, :, :], -1).astype(jnp.int32)


def level_of(stream_key, extent, cuts, least, high):
    factor_of = 1.0
    for dim, shards_of in cuts:
        heights = jax.random.uniform(jax.random.fold_in(jax.random.fold_in(stream_key, 6), dim), (shards_of,), jnp.float32, least / len(cuts), high / len(cuts))
        factor_of = factor_of * jnp.repeat(jnp.exp(heights), extent[dim] // shards_of).reshape((-1,) + (1,) * (len(extent) - 1 - dim))
    return factor_of


def centred(own_key, dims, deviation, most, shards=(), dtype=jnp.bfloat16):
    values = deviation * jax.random.normal(own_key, dims, jnp.float32)
    if shards:
        values = values * level_of(own_key, dims, shards, -0.22, 0.18)
    return jnp.clip(values, -most, most).astype(dtype)


def setup_inputs(seed: int = 0) -> dict:
    seeds = jax.random.split(jax.random.key(seed), 7)
    incoming = centred(seeds[0], (SEGMENTS, NBRICK, VOX, C), 1.0, 6.0, ((0, 12), (1, 64)))
    saved = centred(seeds[1], (SEGMENTS, NBRICK, VOX, C), 1.0, 6.0, ((0, 12), (1, 64)))
    cotangent = centred(seeds[2], (SEGMENTS, NBRICK, VOX, C), 1.0, 6.0, ((0, 12), (1, 64)))
    occupancy = draw_occupancy(jax.random.fold_in(seeds[6], 71), 0)
    neighbours = draw_neighbours(jax.random.fold_in(seeds[6], 71), 0)
    conv_weight = centred(seeds[5], (SEGMENTS, 27, C, C), (12 * C) ** -0.5, 0.15625, ((0, 12),))
    return dict(incoming=incoming, saved=saved, cotangent=cotangent, occupancy=occupancy, neighbours=neighbours, conv_weight=conv_weight)


def voxel_span(step_value):
    if step_value < 0:
        return 3, 4
    if step_value == 0:
        return 0, 4
    return 0, 1


def assemble(source, neighbour_index):
    blocks = source.reshape(source.shape[0], 4, 4, 4, source.shape[-1])
    slab_list = []
    for step_x in (-1, 0, 1):
        row_list = []
        for step_y in (-1, 0, 1):
            fragments = []
            for step_z in (-1, 0, 1):
                offset = 9 * (step_x + 1) + 3 * (step_y + 1) + (step_z + 1)
                low_x, high_x = voxel_span(step_x)
                low_y, high_y = voxel_span(step_y)
                low_z, high_z = voxel_span(step_z)
                fragment = blocks[:, low_x:high_x, low_y:high_y, low_z:high_z, :]
                fragments.append(jnp.take(fragment, neighbour_index[:, offset], axis=0, mode="clip"))
            row_list.append(jnp.concatenate(fragments, axis=3))
        slab_list.append(jnp.concatenate(row_list, axis=2))
    return jnp.concatenate(slab_list, axis=1)


def sparse_conv(source, neighbour_index, weight):
    padded = assemble(source, neighbour_index)
    brick_count = neighbour_index.shape[0]
    channels = source.shape[-1]
    windows = []
    for offset in range(27):
        start_x = offset // 9
        start_y = (offset // 3) % 3
        start_z = offset % 3
        window = padded[:, start_x:start_x + 4, start_y:start_y + 4, start_z:start_z + 4, :]
        windows.append(window.reshape(brick_count * 64, channels))
    stacked = jnp.concatenate(windows, axis=1)
    kernel = weight.reshape(27 * channels, weight.shape[-1])
    accumulated = jnp.dot(stacked, kernel, preferred_element_type=jnp.float32)
    return accumulated.reshape(brick_count, 64, weight.shape[-1])


def silu_slope(values):
    sigmoid_part = jax.nn.sigmoid(values)
    return sigmoid_part * (1.0 + values * (1.0 - sigmoid_part))


def section(operands):
    incoming, saved, cotangent, occupancy, neighbours, conv_weight = operands
    occupied = occupancy.astype(jnp.bfloat16)[:, :, None]
    total_bricks = neighbours.shape[0]
    lookup = jnp.where(neighbours < 0, total_bricks, neighbours).astype(jnp.int32)
    zero_brick = jnp.zeros((1, 64, incoming.shape[-1]), jnp.bfloat16)
    new_input = incoming * occupied
    pre_act = sparse_conv(jnp.concatenate([new_input, zero_brick], axis=0), lookup, conv_weight)
    segment_out = (occupied.astype(jnp.float32) * (new_input.astype(jnp.float32) + jax.nn.silu(pre_act))).astype(jnp.bfloat16)
    old_input = saved * occupied
    masked_grad = cotangent * occupied
    pre_old = sparse_conv(jnp.concatenate([old_input, zero_brick], axis=0), lookup, conv_weight)
    pre_grad = (masked_grad.astype(jnp.float32) * silu_slope(pre_old)).astype(jnp.bfloat16)
    flipped = jnp.transpose(conv_weight[::-1], (0, 2, 1))
    back_term = sparse_conv(jnp.concatenate([pre_grad, zero_brick], axis=0), lookup, flipped)
    input_grad = (occupied.astype(jnp.float32) * (masked_grad.astype(jnp.float32) + back_term)).astype(jnp.bfloat16)
    return segment_out, input_grad


def reference(incoming, saved, cotangent, occupancy, neighbours, conv_weight):
    segment_out, input_grad = lax.map(section, (incoming, saved, cotangent, occupancy, neighbours, conv_weight))
    arrived = jnp.concatenate([jnp.zeros_like(segment_out[:1]), segment_out[:-1]], axis=0)
    returned = jnp.concatenate([input_grad[1:], jnp.zeros_like(input_grad[:1])], axis=0)
    return arrived, returned
```

```python
import functools

import jax
import jax.numpy as jnp
from jax import lax
from jax.experimental import pallas as pl
from jax.experimental.pallas import tpu as pltpu
from jax.sharding import PartitionSpec as P

BF16 = jnp.bfloat16
F32 = jnp.float32
STEPS = (-1, 0, 1)
VMEM_LIMIT = 40 * 1024 * 1024


def source_coordinate(step, c):
    return c if step == 0 else (3 if step < 0 else 0)


def padded_coordinate(step, c):
    return c + 1 if step == 0 else (0 if step < 0 else 5)


def offset_index(ex, ey, ez):
    return 9 * (ex + 1) + 3 * (ey + 1) + (ez + 1)


def gather_plan():
    matrices, plan, mixed = [], [], []
    corners = {-1: [], 1: []}
    for ex in STEPS:
        for ey in STEPS:
            for ez in STEPS:
                steps = (ex, ey, ez)
                zeros = [a for a in range(3) if steps[a] == 0]
                if len(zeros) == 3:
                    continue
                o = offset_index(ex, ey, ez)

                def cell(c):
                    source = [source_coordinate(s, v) for s, v in zip(steps, c)]
                    padded = [padded_coordinate(s, v) for s, v in zip(steps, c)]
                    return (o, tuple(padded), tuple(source))

                if not zeros:
                    corners[ey].append(cell((0, 0, 0)))
                    continue
                along = zeros[0] if len(zeros) == 1 else max(a for a in zeros if a != 1)
                index = len(matrices)
                matrices.append((o,) * 4)
                if along == 1:
                    mixed.append(index)
                outer = [a for a in zeros if a != along]
                for first in range(4) if outer else (0,):
                    cells = []
                    for second in range(4):
                        c = [0, 0, 0]
                        c[along] = second
                        if outer:
                            c[outer[0]] = first
                        cells.append(cell(c))
                    plan.append((index, cells))
    for ey in (-1, 1):
        plan.append((len(matrices), corners[ey]))
        matrices.append(tuple(c[0] for c in corners[ey]))
    return matrices, plan, mixed


MATRICES, PLAN, MIXED = gather_plan()
COUNT = len(MATRICES)


def permutation(mask):
    row = lax.broadcasted_iota(jnp.int32, (256, 256), 0)
    column = lax.broadcasted_iota(jnp.int32, (256, 256), 1)
    hit = column == ((row & 15) * 16 + (row >> 4))
    repeated = jnp.concatenate([mask] * 16, axis=0)
    return jnp.where(hit, repeated, 0.0).astype(BF16)


def rows_mask(occ, block):
    u = lax.broadcasted_iota(jnp.int32, (64, 256), 0)
    column = lax.broadcasted_iota(jnp.int32, (64, 256), 1)
    spread = jnp.where(u == 16 * block + (column & 15), 1.0, 0.0).astype(BF16)
    return jnp.dot(occ, spread, preferred_element_type=F32)


def columns_mask(occ):
    b = lax.broadcasted_iota(jnp.int32, (16, 256), 0)
    column = lax.broadcasted_iota(jnp.int32, (16, 256), 1)
    spread = jnp.where(b == (column & 15), 1.0, 0.0).astype(BF16)
    return lax.dot_general(occ, spread, (((0,), (0,)), ((), ())), preferred_element_type=F32)


def voxel_major(ref, block, matrix):
    rows = ref[:, 16 * block : 16 * block + 16, :].reshape(256, 128)
    return jnp.dot(matrix, rows, preferred_element_type=F32).reshape(16, 16, 128)


def fetch(sources, targets, sems):
    copies = [pltpu.make_async_copy(s, t, sems.at[i]) for i, (s, t) in enumerate(zip(sources, targets))]
    for copy in copies:
        copy.start()
    return copies


def prepare_kernel(saved_hbm, incoming_hbm, occ_hbm, own_old, own_new, send_near, send_far, occ, saved, incoming, sems):
    even = (lax.axis_index("space") & 1) == 0
    copies = fetch((occ_hbm, saved_hbm, incoming_hbm), (occ, saved, incoming), sems)
    for copy in copies:
        copy.wait()
    occupied = occ[...].astype(F32).astype(BF16)
    for block in range(4):
        matrix = permutation(rows_mask(occupied, block))
        old = voxel_major(saved, block, matrix)
        new = voxel_major(incoming, block, matrix)
        part = slice(16 * block, 16 * block + 16)
        own_old[part] = old.astype(BF16)
        own_new[part] = new.astype(BF16)
        low = jnp.concatenate([old[:, :8], new[:, :8]], axis=1)
        high = jnp.concatenate([old[:, 8:], new[:, 8:]], axis=1)
        send_near[part] = jnp.where(even, high, low).astype(BF16)
        send_far[part] = jnp.where(even, low, high).astype(BF16)


def tables_kernel(
    cotangent_hbm, occ_hbm, neighbours_hbm, weight_hbm,
    own_grad, gather, gather_mixed, flipped, weight,
    occ, neighbours, cotangent, sems,
):
    index = lax.axis_index("space")
    even = (index & 1) == 0
    copies = fetch(
        (occ_hbm, neighbours_hbm, cotangent_hbm, weight_hbm), (occ, neighbours, cotangent, weight), sems
    )
    for copy in copies:
        copy.wait()
    occupied = occ[...].astype(F32).astype(BF16)
    for block in range(4):
        matrix = permutation(rows_mask(occupied, block))
        own_grad[16 * block : 16 * block + 16] = voxel_major(cotangent, block, matrix).astype(BF16)
    links = neighbours[...]
    near = links - index * 16
    high_base = jnp.where(even, 64, 128)
    low_base = jnp.where(even, 128, 64)
    outside = (near < 0) | (near >= 16)
    slot = jnp.where(near < 0, near + 8 + low_base, jnp.where(near < 16, near, near - 16 + high_base))
    lane = lax.broadcasted_iota(jnp.int32, (16, 192), 1)

    def one_hot(o, j, extra):
        target = slot[:, o : o + 1] + 16 * j
        if extra:
            target = target + jnp.where(outside[:, o : o + 1], 8, 0)
        target = jnp.where(links[:, o : o + 1] < 0, -1, target)
        return jnp.where(lane == target, 1.0, 0.0)

    for number, offsets in enumerate(MATRICES):
        for variant in range(2):
            rows = [one_hot(o, j, variant == 1) for j, o in enumerate(offsets)]
            gather[variant, number] = jnp.concatenate(rows, axis=0).astype(BF16)
    for place, number in enumerate(MIXED):
        rows = [one_hot(o, j, j >= 2) for j, o in enumerate(MATRICES[number])]
        gather_mixed[place] = jnp.concatenate(rows, axis=0).astype(BF16)
    for o in range(27):
        flipped[128 * o : 128 * o + 128] = weight[128 * (26 - o) : 128 * (27 - o)].T


def voxel_of(cell):
    return 16 * cell[0] + 4 * cell[1] + cell[2]


def fill(padded, own, near, far, gather, variant, gather_mixed=None):
    near = near.at[1 - (lax.axis_index("space") & 1)]
    for x in range(4):
        for y in range(4):
            u = 16 * x + 4 * y
            padded[x + 1, y + 1, 1:5] = own[u : u + 4]
    for number, cells in PLAN:
        sources = [c[2] for c in cells]
        if variant is None:
            halves = [s[1] >> 1 for s in sources]
            tiles = [8 * s[0] + (4 * s[1] + s[2]) % 8 for s in sources]
            if len(set(halves)) == 1:
                matrix = gather[halves[0], number]
            else:
                matrix = gather_mixed[MIXED.index(number)]
        else:
            tiles = [voxel_of(s) for s in sources]
            matrix = gather[variant, number]
        rows = [own[voxel_of(s)] for s in sources] + [near[t] for t in tiles] + [far[t] for t in tiles]
        picked = jnp.dot(matrix, jnp.concatenate(rows, axis=0), preferred_element_type=F32)
        picked = picked.astype(BF16).reshape(4, 16, 128)
        for j, c in enumerate(cells):
            padded[c[1]] = picked[j]


def convolve(padded, weight, x):
    windows = []
    for dx in range(3):
        for dy in range(3):
            for dz in range(3):
                windows.append(padded[x + dx, dy : dy + 4, dz : dz + 4].reshape(256, 128))
    return jnp.dot(jnp.concatenate(windows, axis=1), weight[...], preferred_element_type=F32)


def sigmoid(v):
    return 1.0 / (1.0 + jnp.exp(-v))


def old_kernel(own, near, far, own_grad, gather, weight, grad, send_near, send_far, padded):
    even = (lax.axis_index("space") & 1) == 0
    fill(padded, own, near, far, gather, 0)
    for x in range(4):
        v = convolve(padded, weight, x)
        q = sigmoid(v)
        slope = q * (1.0 + v * (1.0 - q))
        part = slice(16 * x, 16 * x + 16)
        value = own_grad[part].astype(F32) * slope.reshape(16, 16, 128)
        grad[part] = value.astype(BF16)
        low = jnp.concatenate([value[:8, :8], value[8:, :8]], axis=1)
        high = jnp.concatenate([value[:8, 8:], value[8:, 8:]], axis=1)
        here = slice(8 * x, 8 * x + 8)
        send_near[here] = jnp.where(even, high, low).astype(BF16)
        send_far[here] = jnp.where(even, low, high).astype(BF16)


def store_bricks(out, x, value, mask):
    matrix = permutation(mask[16 * x : 16 * x + 16])
    bricks = jnp.dot(matrix, value.astype(BF16), preferred_element_type=F32)
    out[:, 16 * x : 16 * x + 16] = bricks.astype(BF16).reshape(16, 16, 128)


def new_kernel(own, near, far, occ, gather, weight, out, padded):
    mask = columns_mask(occ[...].astype(F32).astype(BF16))
    fill(padded, own, near, far, gather, 1)
    for x in range(4):
        v = convolve(padded, weight, x)
        base = own[16 * x : 16 * x + 16].reshape(256, 128).astype(F32)
        store_bricks(out, x, base + v * sigmoid(v), mask)


def back_kernel(own, near, far, own_grad, occ, gather, gather_mixed, flipped, out, padded):
    mask = columns_mask(occ[...].astype(F32).astype(BF16))
    fill(padded, own, near, far, gather, None, gather_mixed)
    for x in range(4):
        v = convolve(padded, flipped, x)
        base = own_grad[16 * x : 16 * x + 16].reshape(256, 128).astype(F32)
        store_bricks(out, x, base + v, mask)


PADDED = pltpu.VMEM((6, 6, 6, 16, 128), BF16)
BRICKS = pltpu.VMEM((16, 64, 128), BF16)
OCC = pltpu.VMEM((16, 64), jnp.int32)
HBM = pl.BlockSpec(memory_space=pltpu.HBM)
VMEM = pl.BlockSpec(memory_space=pltpu.VMEM)


def call(kernel, shapes, ins, out, scratch=(), flops=0):
    place = pltpu.HBM if out is HBM else pltpu.VMEM
    run = pl.pallas_call(
        kernel,
        out_shape=[place(s, BF16) for s in shapes],
        in_specs=ins,
        out_specs=[out] * len(shapes),
        scratch_shapes=list(scratch),
        compiler_params=pltpu.CompilerParams(vmem_limit_bytes=VMEM_LIMIT),
        cost_estimate=pl.CostEstimate(flops=flops, bytes_accessed=2 << 20, transcendentals=0),
    )

    def placed(*arrays):
        spaces = [pltpu.HBM if spec is HBM else pltpu.VMEM for spec in ins]
        return run(*[pltpu.with_memory_space_constraint(a, m) for a, m in zip(arrays, spaces)])

    return placed


def across(value, count):
    pairs = [(i, i + 1) for i in range(1, count - 1, 2)]
    return lax.ppermute(value, "space", pairs + [(b, a) for a, b in pairs])


def inside(value, count):
    return lax.all_gather(value, "space", axis_index_groups=[[i, i + 1] for i in range(0, count, 2)])


def flush_kernel(source, out, sem):
    copy = pltpu.make_async_copy(source, out, sem)
    copy.start()
    copy.wait()


def per_device(count, sections, incoming, saved, cotangent, occupancy, neighbours, conv_weight):
    incoming, saved, cotangent, occ = incoming[0], saved[0], cotangent[0], occupancy[0]
    links, weight = neighbours[0], conv_weight[0].reshape(27 * 128, 128)
    tile = (64, 16, 128)
    half = (32, 16, 128)
    own_old, own_new, near, far = call(
        prepare_kernel, [tile] * 4, [HBM] * 3, VMEM, [OCC, BRICKS, BRICKS, pltpu.SemaphoreType.DMA((3,))]
    )(saved, incoming, occ)
    far = across(far, count)
    own_grad, gather, gather_mixed, flipped, flat = call(
        tables_kernel,
        [tile, (2, COUNT, 64, 192), (len(MIXED), 64, 192), (27 * 128, 128), (27 * 128, 128)],
        [HBM] * 4,
        VMEM,
        [OCC, pltpu.VMEM((16, 27), jnp.int32), BRICKS, pltpu.SemaphoreType.DMA((4,))],
        flops=1 << 31,
    )(cotangent, occ, links, weight)
    near, own_grad = lax.optimization_barrier((near, own_grad))
    near = inside(near, count)
    grad, grad_near, grad_far = call(
        old_kernel, [tile, half, half], [VMEM] * 6, VMEM, [PADDED], flops=1 << 30
    )(own_old, near, far, own_grad, gather, flat)
    grad_far = across(grad_far, count)
    grad_near = inside(grad_near, count)
    (out,) = call(new_kernel, [(16, 64, 128)], [VMEM] * 6, VMEM, [PADDED], flops=1 << 30)(
        own_new, near, far, occ, gather, flat
    )
    arrived = lax.ppermute(out[None], "segment", [(s, s + 1) for s in range(sections - 1)])
    (back,) = call(back_kernel, [(16, 64, 128)], [VMEM] * 8, VMEM, [PADDED], flops=1 << 30)(
        grad, grad_near, grad_far, own_grad, occ, gather, gather_mixed, flipped
    )
    returned = lax.ppermute(back[None], "segment", [(s + 1, s) for s in range(sections - 1)])
    (arrived,) = call(flush_kernel, [(1, 16, 64, 128)], [VMEM], HBM, [pltpu.SemaphoreType.DMA])(arrived)
    return arrived, returned


def solution(mesh):
    brick = P("segment", "space", None, None)
    index = P("segment", "space", None)
    return jax.shard_map(
        functools.partial(per_device, mesh.shape["space"], mesh.shape["segment"]),
        mesh=mesh,
        in_specs=(brick, brick, brick, index, index, P("segment", None, None, None)),
        out_specs=(brick, brick),
        check_vma=False,
    )
```

```python
import functools

import jax
import jax.numpy as jnp
from jax import lax
from jax.experimental import pallas as pl
from jax.experimental.pallas import tpu as pltpu
from jax.sharding import PartitionSpec as P

BF16 = jnp.bfloat16
F32 = jnp.float32
STEPS = (-1, 0, 1)
VMEM_LIMIT = 40 * 1024 * 1024


def source_coordinate(step, c):
    return c if step == 0 else (3 if step < 0 else 0)


def padded_coordinate(step, c):
    return c + 1 if step == 0 else (0 if step < 0 else 5)


def offset_index(ex, ey, ez):
    return 9 * (ex + 1) + 3 * (ey + 1) + (ez + 1)


def gather_plan():
    matrices, plan, mixed = [], [], []
    corners = {-1: [], 1: []}
    for ex in STEPS:
        for ey in STEPS:
            for ez in STEPS:
                steps = (ex, ey, ez)
                zeros = [a for a in range(3) if steps[a] == 0]
                if len(zeros) == 3:
                    continue
                o = offset_index(ex, ey, ez)

                def cell(c):
                    source = [source_coordinate(s, v) for s, v in zip(steps, c)]
                    padded = [padded_coordinate(s, v) for s, v in zip(steps, c)]
                    return (o, tuple(padded), tuple(source))

                if not zeros:
                    corners[ey].append(cell((0, 0, 0)))
                    continue
                along = zeros[0] if len(zeros) == 1 else max(a for a in zeros if a != 1)
                index = len(matrices)
                matrices.append((o,) * 4)
                if along == 1:
                    mixed.append(index)
                outer = [a for a in zeros if a != along]
                groups = []
                for first in range(4) if outer else (0,):
                    cells = []
                    for second in range(4):
                        c = [0, 0, 0]
                        c[along] = second
                        if outer:
                            c[outer[0]] = first
                        cells.append(cell(c))
                    groups.append(cells)
                plan.append((index, groups))
    for ey in (-1, 1):
        plan.append((len(matrices), [corners[ey]]))
        matrices.append(tuple(c[0] for c in corners[ey]))
    return matrices, plan, mixed


MATRICES, PLAN, MIXED = gather_plan()
COUNT = len(MATRICES)


def voxel_major(ref, mask, block):
    part = slice(16 * block, 16 * block + 16)
    return jnp.swapaxes(ref[:, part, :].astype(F32), 0, 1) * mask[part].astype(F32)


def fetch(sources, targets, sems):
    copies = [pltpu.make_async_copy(s, t, sems.at[i]) for i, (s, t) in enumerate(zip(sources, targets))]
    for copy in copies:
        copy.start()
    return copies


def prepare_kernel(saved_hbm, incoming_hbm, occ_hbm, own_old, own_new, send_near, send_far, mask, occ, saved, incoming, sems):
    even = (lax.axis_index("space") & 1) == 0
    copies = fetch((occ_hbm, saved_hbm, incoming_hbm), (occ, saved, incoming), sems)
    copies[0].wait()
    occupied = occ[...].astype(F32)
    for u in range(64):
        mask[u] = jnp.broadcast_to(occupied[:, u : u + 1], (16, 128)).astype(BF16)
    copies[1].wait()
    copies[2].wait()
    for block in range(4):
        old = voxel_major(saved, mask, block)
        new = voxel_major(incoming, mask, block)
        part = slice(16 * block, 16 * block + 16)
        own_old[part] = old.astype(BF16)
        own_new[part] = new.astype(BF16)
        low = jnp.concatenate([old[:, :8], new[:, :8]], axis=1)
        high = jnp.concatenate([old[:, 8:], new[:, 8:]], axis=1)
        send_near[part] = jnp.where(even, high, low).astype(BF16)
        send_far[part] = jnp.where(even, low, high).astype(BF16)


def widened(out, kernel_of):
    for k in range(9):
        blocks = [kernel_of(3 * k + i) for i in range(3)]
        zero = jnp.zeros_like(blocks[0])
        for j in range(4):
            row = slice(128 * (4 * k + j), 128 * (4 * k + j + 1))
            out[row, :128] = blocks[j] if j < 3 else zero
            out[row, 128:] = blocks[j - 1] if j > 0 else zero


def tables_kernel(
    cotangent_hbm, neighbours_hbm, weight_hbm, mask,
    own_grad, gather, gather_mixed, wide, flipped,
    neighbours, cotangent, weight, sems,
):
    index = lax.axis_index("space")
    even = (index & 1) == 0
    copies = fetch(
        (neighbours_hbm, cotangent_hbm, weight_hbm), (neighbours, cotangent, weight), sems
    )
    copies[0].wait()
    links = neighbours[...]
    near = links - index * 16
    high_base = jnp.where(even, 64, 128)
    low_base = jnp.where(even, 128, 64)
    outside = (near < 0) | (near >= 16)
    slot = jnp.where(near < 0, near + 8 + low_base, jnp.where(near < 16, near, near - 16 + high_base))
    slot = jnp.where(links < 0, -1024, slot)
    moved = jnp.where(outside, slot + 8, slot)
    lane = lax.broadcasted_iota(jnp.int32, (64, 192), 1) - 16 * (
        lax.broadcasted_iota(jnp.int32, (64, 192), 0) >> 4
    )

    def one_hot(offsets, extra):
        columns = [(moved if e else slot)[:, o : o + 1] for o, e in zip(offsets, extra)]
        return jnp.where(lane == jnp.concatenate(columns, axis=0), 1.0, 0.0).astype(BF16)

    for number, offsets in enumerate(MATRICES):
        gather[0, number] = one_hot(offsets, (False,) * 4)
        gather[1, number] = one_hot(offsets, (True,) * 4)
    for place, number in enumerate(MIXED):
        gather_mixed[place] = one_hot(MATRICES[number], (False, False, True, True))
    copies[1].wait()
    for block in range(4):
        own_grad[16 * block : 16 * block + 16] = voxel_major(cotangent, mask, block).astype(BF16)
    copies[2].wait()
    widened(wide, lambda o: weight[o])
    widened(flipped, lambda o: weight[26 - o].T)


def voxel_of(cell):
    return 16 * cell[0] + 4 * cell[1] + cell[2]


def fill(padded, own, near, far, gather, variant, gather_mixed=None):
    near = near.at[1 - (lax.axis_index("space") & 1)]
    for x in range(4):
        for y in range(4):
            u = 16 * x + 4 * y
            padded[x + 1, y + 1, 1:5] = own[u : u + 4]
    for number, groups in PLAN:
        columns = []
        for cells in groups:
            sources = [c[2] for c in cells]
            tiles = [voxel_of(s) for s in sources]
            if variant is None:
                halves = [s[1] >> 1 for s in sources]
                tiles = [8 * s[0] + (4 * s[1] + s[2]) % 8 for s in sources]
            rows = [own[voxel_of(s)] for s in sources] + [near[t] for t in tiles] + [far[t] for t in tiles]
            columns.append((jnp.concatenate(rows, axis=0), halves if variant is None else [variant] * 4, cells))
        kinds = sorted({tuple(c[1]) for c in columns})
        for kind in kinds:
            chosen = [c for c in columns if tuple(c[1]) == kind]
            matrix = gather[kind[0], number] if len(set(kind)) == 1 else gather_mixed[MIXED.index(number)]
            picked = jnp.dot(
                matrix, jnp.concatenate([c[0] for c in chosen], axis=1), preferred_element_type=F32
            ).astype(BF16)
            for i, (_, _, cells) in enumerate(chosen):
                part = picked[:, 128 * i : 128 * i + 128].reshape(4, 16, 128)
                for j, c in enumerate(cells):
                    padded[c[1]] = part[j]


def convolve(padded, weight, x):
    windows = []
    for dx in range(3):
        for dy in range(3):
            for j in range(4):
                windows.append(padded[x + dx : x + dx + 2, dy : dy + 4, j : j + 3 : 2].reshape(256, 128))
    both = jnp.dot(jnp.concatenate(windows, axis=1), weight[...], preferred_element_type=F32)
    halves = [both[:, 128 * h : 128 * h + 128].reshape(16, 1, 16, 128) for h in range(2)]
    return jnp.concatenate(halves, axis=1).reshape(32, 16, 128)


def sigmoid(v):
    return 1.0 / (1.0 + jnp.exp(-v))


def old_kernel(own, near, far, own_grad, gather, weight, grad, send_near, send_far, padded):
    even = (lax.axis_index("space") & 1) == 0
    fill(padded, own, near, far, gather, 0)
    for pair in range(2):
        v = convolve(padded, weight, 2 * pair)
        q = sigmoid(v)
        slope = q * (1.0 + v * (1.0 - q))
        part = slice(32 * pair, 32 * pair + 32)
        value = own_grad[part].astype(F32) * slope
        grad[part] = value.astype(BF16)
        for h in range(2):
            first, second = value[16 * h : 16 * h + 8], value[16 * h + 8 : 16 * h + 16]
            low = jnp.concatenate([first[:, :8], second[:, :8]], axis=1)
            high = jnp.concatenate([first[:, 8:], second[:, 8:]], axis=1)
            here = slice(16 * pair + 8 * h, 16 * pair + 8 * h + 8)
            send_near[here] = jnp.where(even, high, low).astype(BF16)
            send_far[here] = jnp.where(even, low, high).astype(BF16)


def store_bricks(out, pair, value, mask):
    part = slice(32 * pair, 32 * pair + 32)
    out[:, part] = jnp.swapaxes(value * mask[part].astype(F32), 0, 1).astype(BF16)


def new_kernel(own, near, far, mask, gather, weight, out, padded):
    fill(padded, own, near, far, gather, 1)
    for pair in range(2):
        v = convolve(padded, weight, 2 * pair)
        base = own[32 * pair : 32 * pair + 32].astype(F32)
        store_bricks(out, pair, base + v * sigmoid(v), mask)


def back_kernel(own, near, far, own_grad, mask, gather, gather_mixed, flipped, out, padded):
    fill(padded, own, near, far, gather, None, gather_mixed)
    for pair in range(2):
        v = convolve(padded, flipped, 2 * pair)
        base = own_grad[32 * pair : 32 * pair + 32].astype(F32)
        store_bricks(out, pair, base + v, mask)


PADDED = pltpu.VMEM((6, 6, 6, 16, 128), BF16)
BRICKS = pltpu.VMEM((16, 64, 128), BF16)
OCC = pltpu.VMEM((16, 64), jnp.int32)
HBM = pl.BlockSpec(memory_space=pltpu.HBM)
VMEM = pl.BlockSpec(memory_space=pltpu.VMEM)


def call(kernel, shapes, ins, out, scratch=(), flops=0):
    place = pltpu.HBM if out is HBM else pltpu.VMEM
    run = pl.pallas_call(
        kernel,
        out_shape=[place(s, BF16) for s in shapes],
        in_specs=ins,
        out_specs=[out] * len(shapes),
        scratch_shapes=list(scratch),
        compiler_params=pltpu.CompilerParams(vmem_limit_bytes=VMEM_LIMIT),
        cost_estimate=pl.CostEstimate(flops=flops, bytes_accessed=2 << 20, transcendentals=0),
    )

    def placed(*arrays):
        spaces = [pltpu.HBM if spec is HBM else pltpu.VMEM for spec in ins]
        return run(*[pltpu.with_memory_space_constraint(a, m) for a, m in zip(arrays, spaces)])

    return placed


def across(value, count):
    pairs = [(i, i + 1) for i in range(1, count - 1, 2)]
    return lax.ppermute(value, "space", pairs + [(b, a) for a, b in pairs])


def inside(value, count):
    return lax.all_gather(value, "space", axis_index_groups=[[i, i + 1] for i in range(0, count, 2)])


def flush_kernel(source, out, sem):
    copy = pltpu.make_async_copy(source, out, sem)
    copy.start()
    copy.wait()


def per_device(count, sections, incoming, saved, cotangent, occupancy, neighbours, conv_weight):
    incoming, saved, cotangent, occ = incoming[0], saved[0], cotangent[0], occupancy[0]
    links, weight = neighbours[0], conv_weight[0]
    tile = (64, 16, 128)
    half = (32, 16, 128)
    own_old, own_new, near, far, mask = call(
        prepare_kernel, [tile] * 5, [HBM] * 3, VMEM, [OCC, BRICKS, BRICKS, pltpu.SemaphoreType.DMA((3,))]
    )(saved, incoming, occ)
    far = across(far, count)
    own_grad, gather, gather_mixed, wide, flipped = call(
        tables_kernel,
        [tile, (2, COUNT, 64, 192), (len(MIXED), 64, 192), (36 * 128, 256), (36 * 128, 256)],
        [HBM] * 3 + [VMEM],
        VMEM,
        [
            pltpu.VMEM((16, 27), jnp.int32),
            BRICKS,
            pltpu.VMEM((27, 128, 128), BF16),
            pltpu.SemaphoreType.DMA((3,)),
        ],
        flops=1 << 31,
    )(cotangent, links, weight, mask)
    near, own_grad = lax.optimization_barrier((near, own_grad))
    near = inside(near, count)
    grad, grad_near, grad_far = call(
        old_kernel, [tile, half, half], [VMEM] * 6, VMEM, [PADDED], flops=1 << 30
    )(own_old, near, far, own_grad, gather, wide)
    grad_far = across(grad_far, count)
    grad_near = inside(grad_near, count)
    (out,) = call(new_kernel, [(16, 64, 128)], [VMEM] * 6, VMEM, [PADDED], flops=1 << 30)(
        own_new, near, far, mask, gather, wide
    )
    arrived = lax.ppermute(out[None], "segment", [(s, s + 1) for s in range(sections - 1)])
    (back,) = call(back_kernel, [(16, 64, 128)], [VMEM] * 8, VMEM, [PADDED], flops=1 << 30)(
        grad, grad_near, grad_far, own_grad, mask, gather, gather_mixed, flipped
    )
    returned = lax.ppermute(back[None], "segment", [(s + 1, s) for s in range(sections - 1)])
    (arrived,) = call(flush_kernel, [(1, 16, 64, 128)], [VMEM], HBM, [pltpu.SemaphoreType.DMA])(arrived)
    return arrived, returned


def solution(mesh):
    brick = P("segment", "space", None, None)
    index = P("segment", "space", None)
    return jax.shard_map(
        functools.partial(per_device, mesh.shape["space"], mesh.shape["segment"]),
        mesh=mesh,
        in_specs=(brick, brick, brick, index, index, P("segment", None, None, None)),
        out_specs=(brick, brick),
        check_vma=False,
    )
```

```python
import functools

import jax
import jax.numpy as jnp
from jax import lax
from jax.experimental import pallas as pl
from jax.experimental.pallas import tpu as pltpu
from jax.sharding import PartitionSpec as P

BF16 = jnp.bfloat16
F32 = jnp.float32
STEPS = (-1, 0, 1)
VMEM_LIMIT = 40 * 1024 * 1024


def source_coordinate(step, c):
    return c if step == 0 else (3 if step < 0 else 0)


def padded_coordinate(step, c):
    return c + 1 if step == 0 else (0 if step < 0 else 5)


def gather_plan():
    matrices, plan = [], []
    corners = {-1: [], 1: []}
    centre = None
    for o in range(27):
        steps = (o // 9 - 1, o // 3 % 3 - 1, o % 3 - 1)
        zeros = [a for a in range(3) if steps[a] == 0]

        def cell(c):
            source = [source_coordinate(s, v) for s, v in zip(steps, c)]
            padded = [padded_coordinate(s, v) for s, v in zip(steps, c)]
            return tuple(padded), 16 * source[0] + 4 * source[1] + source[2]

        if not zeros:
            corners[steps[1]].append((o, cell((0, 0, 0))))
            continue
        along, outer = zeros[-1], zeros[:-1]
        groups = []
        for first in range(4 ** len(outer)):
            c = [0, 0, 0]
            for a in outer:
                c[a] = first % 4
                first //= 4
            cells = []
            for second in range(4):
                c[along] = second
                cells.append(cell(c))
            groups.append(cells)
        if len(zeros) == 3:
            centre = ((o,) * 4, groups)
        else:
            matrices.append((o,) * 4)
            plan.append(groups)
    for side in (-1, 1):
        matrices.append(tuple(o for o, _ in corners[side]))
        plan.append([[c for _, c in corners[side]]])
    matrices.append(centre[0])
    plan.append(centre[1])
    return matrices, plan


MATRICES, PLAN = gather_plan()
COUNT = len(MATRICES)
LINKS = 128


def fetch(sources, targets, sems):
    copies = [pltpu.make_async_copy(s, t, sems.at[i]) for i, (s, t) in enumerate(zip(sources, targets))]
    for copy in copies:
        copy.start()
    return copies


def is_even():
    return (lax.axis_index("space") & 1) == 0


def voxel_major(ref, mask, block):
    part = slice(16 * block, 16 * block + 16)
    return jnp.swapaxes(ref[:, part, :].astype(F32), 0, 1) * mask[part].astype(F32)


def prepare_kernel(
    saved_hbm, cotangent_hbm, incoming_hbm, occ_hbm, links_hbm,
    send_near, send_far, own_new, own_grad, mask,
    occ, links, saved, cotangent, incoming, sems,
):
    even = is_even()
    copies = fetch(
        (occ_hbm, links_hbm, saved_hbm, cotangent_hbm, incoming_hbm), (occ, links, saved, cotangent, incoming), sems
    )
    copies[0].wait()
    occupied = occ[...].astype(F32)
    for u in range(64):
        mask[u] = jnp.broadcast_to(occupied[:, u : u + 1], (16, 128)).astype(BF16)
    copies[1].wait()
    named = links[...]
    first = 16 * lax.axis_index("space") + lax.broadcasted_iota(jnp.int32, (16, 27), 0)
    code = jnp.where(named < 0, 0, named - first + 8).astype(F32)
    code = jnp.concatenate([code, jnp.zeros((16, 101), F32)], axis=1).astype(BF16)
    send_near[LINKS] = code
    send_far[LINKS] = code
    for copy in copies[2:]:
        copy.wait()
    for block in range(4):
        part = slice(16 * block, 16 * block + 16)
        after = slice(64 + 16 * block, 64 + 16 * block + 16)
        old = voxel_major(saved, mask, block).astype(BF16)
        send_near[part] = old
        send_far[part] = old
        grad = voxel_major(cotangent, mask, block)
        new = voxel_major(incoming, mask, block)
        own_grad[part] = grad.astype(BF16)
        own_new[part] = new.astype(BF16)
        low = jnp.concatenate([grad[:, :8], new[:, :8]], axis=1)
        high = jnp.concatenate([grad[:, 8:], new[:, 8:]], axis=1)
        send_near[after] = jnp.where(even, high, low).astype(BF16)
        send_far[after] = jnp.where(even, low, high).astype(BF16)


def one_hot(slot, offsets, sources):
    shape = (64, 64 * sources)
    lane = lax.broadcasted_iota(jnp.int32, shape, 1) - 16 * (lax.broadcasted_iota(jnp.int32, shape, 0) >> 4)
    columns = jnp.concatenate([slot[:, o : o + 1] for o in offsets], axis=0)
    return jnp.where(lane == columns, 1.0, 0.0).astype(BF16)


def widened(out, kernel_of):
    for k in range(9):
        blocks = [kernel_of(3 * k + i) for i in range(3)]
        zero = jnp.zeros_like(blocks[0])
        for j in range(4):
            row = slice(128 * (4 * k + j), 128 * (4 * k + j + 1))
            out[row, :128] = blocks[j] if j < 3 else zero
            out[row, 128:] = blocks[j - 1] if j > 0 else zero


def decoded(tile, first):
    code = tile.astype(F32)[:, :27].astype(jnp.int32)
    return code - 8 + first, code > 0


def tables_kernel(own, weight_hbm, gather_new, gather_back, wide, flipped, weight, sems):
    even = is_even()
    (copy,) = fetch((weight_hbm,), (weight,), sems)
    named, present = decoded(own[LINKS], lax.broadcasted_iota(jnp.int32, (16, 27), 0))
    outside = (named < 0) | (named >= 16)
    near_side = (named >= 8) == even
    row = named & 7
    slot = jnp.where(outside, row + jnp.where(near_side, 72, 136), named)
    slot = jnp.where(present, slot, -1024)
    for number, offsets in enumerate(MATRICES[:-1]):
        gather_new[number] = one_hot(slot, offsets, 3)
    slot = row + jnp.where(outside, 8, 0) + jnp.where(near_side, 0, 64)
    slot = jnp.where(present, slot, -1024)
    for number, offsets in enumerate(MATRICES):
        gather_back[number] = one_hot(slot, offsets, 2)
    copy.wait()
    widened(wide, lambda o: weight[o])
    widened(flipped, lambda o: weight[26 - o].T)


def fill(padded, sources, gather, count):
    for number, groups in enumerate(PLAN[:count]):
        matrix = gather(number)
        for start in range(0, len(groups), 4):
            chosen = groups[start : start + 4]
            columns = [
                jnp.concatenate([rows(u) for rows in sources for _, u in cells], axis=0) for cells in chosen
            ]
            picked = jnp.dot(
                matrix, jnp.concatenate(columns, axis=1), preferred_element_type=F32
            ).astype(BF16)
            for i, cells in enumerate(chosen):
                part = picked[:, 128 * i : 128 * i + 128].reshape(4, 16, 128)
                for j, (place, _) in enumerate(cells):
                    padded[place] = part[j]


def convolve(padded, weight, x):
    windows = []
    for dx in range(3):
        for dy in range(3):
            for j in range(4):
                windows.append(padded[x + dx : x + dx + 2, dy : dy + 4, j : j + 3 : 2].reshape(256, 128))
    both = jnp.dot(jnp.concatenate(windows, axis=1), weight[...], preferred_element_type=F32)
    halves = [both[:, 128 * h : 128 * h + 128].reshape(16, 1, 16, 128) for h in range(2)]
    return jnp.concatenate(halves, axis=1).reshape(32, 16, 128)


def sigmoid(v):
    return 1.0 / (1.0 + jnp.exp(-v))


def old_kernel(far, own, other, own_grad, wide, grad, padded):
    even = is_even()
    high = even != far
    row = lax.broadcasted_iota(jnp.int32, (16, 27), 0)
    own_named, own_present = decoded(own[LINKS], row)
    near_named, near_present = decoded(other[LINKS], row + jnp.where(high, 16, -16))

    def sides(mine, theirs):
        return jnp.concatenate(
            [jnp.where(high, mine[8:], mine[:8]), jnp.where(high, theirs[:8], theirs[8:])], axis=0
        )

    own_named = jnp.where(own_present, own_named, -1024)
    near_named = jnp.where(near_present, near_named, -1024)
    named = sides(own_named, near_named)
    slot = jnp.where((named >= 0) & (named < 16), named, (named & 15) + 64)
    slot = jnp.where(named == -1024, -1024, slot)
    fill(
        padded,
        (lambda u: own[u], lambda u: other[u]),
        lambda number: one_hot(slot, MATRICES[number], 2),
        COUNT,
    )
    for pair in range(2):
        v = convolve(padded, wide, 2 * pair)
        q = sigmoid(v)
        slope = q * (1.0 + v * (1.0 - q))
        part = slice(32 * pair, 32 * pair + 32)
        mine = own_grad[part].astype(F32)
        theirs = other[64 + 32 * pair : 96 + 32 * pair].astype(F32)
        masked = jnp.concatenate([jnp.where(high, mine[:, 8:], mine[:, :8]), theirs[:, :8]], axis=1)
        grad[part] = (masked * slope).astype(BF16)


def old_near_kernel(own, near, own_grad, wide, grad, padded):
    old_kernel(False, own, near.at[1 - (lax.axis_index("space") & 1)], own_grad, wide, grad, padded)


def old_far_kernel(own, far, own_grad, wide, grad, padded):
    old_kernel(True, own, far, own_grad, wide, grad, padded)


def store_bricks(out, pair, value, mask):
    part = slice(32 * pair, 32 * pair + 32)
    out[:, part] = jnp.swapaxes(value * mask[part].astype(F32), 0, 1).astype(BF16)


def new_kernel(own, near, far, mask, gather, wide, out, padded):
    near = near.at[1 - (lax.axis_index("space") & 1)]
    for x in range(4):
        for y in range(4):
            u = 16 * x + 4 * y
            padded[x + 1, y + 1, 1:5] = own[u : u + 4]
    fill(
        padded,
        (lambda u: own[u], lambda u: near[64 + u], lambda u: far[64 + u]),
        lambda number: gather[number],
        COUNT - 1,
    )
    for pair in range(2):
        v = convolve(padded, wide, 2 * pair)
        base = own[32 * pair : 32 * pair + 32].astype(F32)
        store_bricks(out, pair, base + v * sigmoid(v), mask)


def back_kernel(near, far, own_grad, mask, gather, flipped, out, padded):
    fill(padded, (lambda u: near[u], lambda u: far[u]), lambda number: gather[number], COUNT)
    for pair in range(2):
        v = convolve(padded, flipped, 2 * pair)
        base = own_grad[32 * pair : 32 * pair + 32].astype(F32)
        store_bricks(out, pair, base + v, mask)


PADDED = pltpu.VMEM((6, 6, 6, 16, 128), BF16)
BRICKS = pltpu.VMEM((16, 64, 128), BF16)
OCC = pltpu.VMEM((16, 64), jnp.int32)
HBM = pl.BlockSpec(memory_space=pltpu.HBM)
VMEM = pl.BlockSpec(memory_space=pltpu.VMEM)


def call(kernel, shapes, ins, out, scratch=(), flops=0):
    place = pltpu.HBM if out is HBM else pltpu.VMEM
    run = pl.pallas_call(
        kernel,
        out_shape=[place(s, BF16) for s in shapes],
        in_specs=ins,
        out_specs=[out] * len(shapes),
        scratch_shapes=list(scratch),
        compiler_params=pltpu.CompilerParams(vmem_limit_bytes=VMEM_LIMIT),
        cost_estimate=pl.CostEstimate(flops=flops, bytes_accessed=2 << 20, transcendentals=0),
    )

    def placed(*arrays):
        spaces = [pltpu.HBM if spec is HBM else pltpu.VMEM for spec in ins]
        return run(*[pltpu.with_memory_space_constraint(a, m) for a, m in zip(arrays, spaces)])

    return placed


def across(value, count):
    pairs = [(i, i + 1) for i in range(1, count - 1, 2)]
    return lax.ppermute(value, "space", pairs + [(b, a) for a, b in pairs])


def inside(value, count):
    return lax.all_gather(value, "space", axis_index_groups=[[i, i + 1] for i in range(0, count, 2)])


def flush_kernel(source, out, sem):
    copy = pltpu.make_async_copy(source, out, sem)
    copy.start()
    copy.wait()


def per_device(count, sections, incoming, saved, cotangent, occupancy, neighbours, conv_weight):
    tile = (64, 16, 128)
    payload = (LINKS + 1, 16, 128)
    send_near, send_far, own_new, own_grad, mask = call(
        prepare_kernel,
        [payload, payload, tile, tile, tile],
        [HBM] * 5,
        VMEM,
        [
            pltpu.VMEM((16, 64), jnp.int32),
            pltpu.VMEM((16, 27), jnp.int32),
            BRICKS,
            BRICKS,
            BRICKS,
            pltpu.SemaphoreType.DMA((5,)),
        ],
    )(saved[0], cotangent[0], incoming[0], occupancy[0], neighbours[0])
    far = across(send_far, count)
    gather_new, gather_back, wide, flipped = call(
        tables_kernel,
        [(COUNT - 1, 64, 192), (COUNT, 64, 128), (36 * 128, 256), (36 * 128, 256)],
        [VMEM, HBM],
        VMEM,
        [pltpu.VMEM((27, 128, 128), BF16), pltpu.SemaphoreType.DMA((1,))],
        flops=1 << 31,
    )(send_near, conv_weight[0])
    send_near, wide = lax.optimization_barrier((send_near, wide))
    near = inside(send_near, count)
    (grad_near,) = call(old_near_kernel, [tile], [VMEM] * 4, VMEM, [PADDED], flops=1 << 30)(
        send_near, near, own_grad, wide
    )
    (out,) = call(new_kernel, [(16, 64, 128)], [VMEM] * 6, VMEM, [PADDED], flops=1 << 30)(
        own_new, near, far, mask, gather_new, wide
    )
    arrived = lax.ppermute(out[None], "segment", [(s, s + 1) for s in range(sections - 1)])
    (grad_far,) = call(old_far_kernel, [tile], [VMEM] * 4, VMEM, [PADDED], flops=1 << 30)(
        send_near, far, own_grad, wide
    )
    (back,) = call(back_kernel, [(16, 64, 128)], [VMEM] * 6, VMEM, [PADDED], flops=1 << 30)(
        grad_near, grad_far, own_grad, mask, gather_back, flipped
    )
    returned = lax.ppermute(back[None], "segment", [(s + 1, s) for s in range(sections - 1)])
    (arrived,) = call(flush_kernel, [(1, 16, 64, 128)], [VMEM], HBM, [pltpu.SemaphoreType.DMA])(arrived)
    return arrived, returned


def solution(mesh):
    brick = P("segment", "space", None, None)
    index = P("segment", "space", None)
    return jax.shard_map(
        functools.partial(per_device, mesh.shape["space"], mesh.shape["segment"]),
        mesh=mesh,
        in_specs=(brick, brick, brick, index, index, P("segment", None, None, None)),
        out_specs=(brick, brick),
        check_vma=False,
    )
```

```python
import functools

import jax
import jax.numpy as jnp
from jax import lax
from jax.experimental import pallas as pl
from jax.experimental.pallas import tpu as pltpu
from jax.sharding import PartitionSpec as P

BF16 = jnp.bfloat16
F32 = jnp.float32
STEPS = (-1, 0, 1)
VMEM_LIMIT = 40 * 1024 * 1024


def source_coordinate(step, c):
    return c if step == 0 else (3 if step < 0 else 0)


def padded_coordinate(step, c):
    return c + 1 if step == 0 else (0 if step < 0 else 5)


def gather_plan():
    matrices, plan = [], []
    corners = {-1: [], 1: []}
    centre = None
    for o in range(27):
        steps = (o // 9 - 1, o // 3 % 3 - 1, o % 3 - 1)
        zeros = [a for a in range(3) if steps[a] == 0]

        def cell(c):
            source = [source_coordinate(s, v) for s, v in zip(steps, c)]
            padded = [padded_coordinate(s, v) for s, v in zip(steps, c)]
            return tuple(padded), 16 * source[0] + 4 * source[1] + source[2]

        if not zeros:
            corners[steps[1]].append((o, cell((0, 0, 0))))
            continue
        along, outer = zeros[-1], zeros[:-1]
        groups = []
        for first in range(4 ** len(outer)):
            c = [0, 0, 0]
            for a in outer:
                c[a] = first % 4
                first //= 4
            cells = []
            for second in range(4):
                c[along] = second
                cells.append(cell(c))
            groups.append(cells)
        if len(zeros) == 3:
            centre = ((o,) * 4, groups)
        else:
            matrices.append((o,) * 4)
            plan.append(groups)
    for side in (-1, 1):
        matrices.append(tuple(o for o, _ in corners[side]))
        plan.append([[c for _, c in corners[side]]])
    matrices.append(centre[0])
    plan.append(centre[1])
    return matrices, plan


MATRICES, PLAN = gather_plan()
COUNT = len(MATRICES)
TAIL = 62
LINKS = 64 + TAIL


def fetch(sources, targets, sems):
    copies = [pltpu.make_async_copy(s, t, sems.at[i]) for i, (s, t) in enumerate(zip(sources, targets))]
    for copy in copies:
        copy.start()
    return copies


def is_even():
    return (lax.axis_index("space") & 1) == 0


def voxel_major(ref, mask, block):
    part = slice(16 * block, 16 * block + 16)
    return jnp.swapaxes(ref[:, part, :].astype(F32), 0, 1) * mask[part].astype(F32)


def rows8():
    return lax.broadcasted_iota(jnp.int32, (8, 128), 0)


def stored_tail(rows, tail):
    packed = []
    for t in range(14):
        row = t % 7 + 1
        packed.append(jnp.where(rows8() == 0, pltpu.roll(tail[t // 7], 8 - row, 0), rows[t])[None])
    return jnp.concatenate(packed + [rows[14:]], axis=0)


def read_tail(payload):
    tiles = []
    for which in range(2):
        parts = [jnp.zeros((8, 128), F32)] * 2
        for row in range(1, 8):
            tile = payload[64 + 7 * which + row - 1].astype(F32)
            parts = [
                jnp.where(rows8() == row, pltpu.roll(tile[8 * h : 8 * h + 8], row, 0), parts[h]) for h in range(2)
            ]
        tiles.append(jnp.concatenate(parts, axis=0))
    return tiles


def prepare_kernel(
    saved_hbm, cotangent_hbm, incoming_hbm, occ_hbm, links_hbm,
    send_near, send_far, own_new, own_grad, mask,
    occ, links, saved, cotangent, incoming, sems,
):
    even = is_even()
    copies = fetch(
        (occ_hbm, links_hbm, saved_hbm, cotangent_hbm, incoming_hbm), (occ, links, saved, cotangent, incoming), sems
    )
    copies[0].wait()
    occupied = occ[...].astype(F32)
    for u in range(64):
        mask[u] = jnp.broadcast_to(occupied[:, u : u + 1], (16, 128)).astype(BF16)
    copies[1].wait()
    named = links[...]
    first = 16 * lax.axis_index("space") + lax.broadcasted_iota(jnp.int32, (16, 27), 0)
    code = jnp.where(named < 0, 0, named - first + 8).astype(F32)
    code = jnp.concatenate([code, jnp.zeros((16, 101), F32)], axis=1).astype(BF16)
    send_near[LINKS] = code
    send_far[LINKS] = code
    for copy in copies[2:]:
        copy.wait()
    tails = {}
    for block in (3, 1, 2, 0):
        part = slice(16 * block, 16 * block + 16)
        old = voxel_major(saved, mask, block).astype(BF16)
        send_near[part] = old
        send_far[part] = old
        grad = voxel_major(cotangent, mask, block)
        new = voxel_major(incoming, mask, block)
        own_grad[part] = grad.astype(BF16)
        own_new[part] = new.astype(BF16)
        low = [pltpu.roll(v[:, :8], 1, 1) for v in (grad, new)]
        high = [v[:, 8:] for v in (grad, new)]
        for side, send in enumerate((send_near, send_far)):
            rows = [jnp.where(even == (side == 0), h, l) for h, l in zip(high, low)]
            if block == 3:
                tails[side] = [(r[14], r[15]) for r in rows]
                rows = [r[:14] for r in rows]
            if block == 0:
                rows = [stored_tail(r, tail) for r, tail in zip(rows, tails[side])]
            size = rows[0].shape[0]
            send[64 + 16 * block : 64 + 16 * block + size] = jnp.concatenate(rows, axis=1).astype(BF16)


def one_hot(slot, offsets, sources):
    shape = (64, 64 * sources)
    lane = lax.broadcasted_iota(jnp.int32, shape, 1) - 16 * (lax.broadcasted_iota(jnp.int32, shape, 0) >> 4)
    columns = jnp.concatenate([slot[:, o : o + 1] for o in offsets], axis=0)
    return jnp.where(lane == columns, 1.0, 0.0).astype(BF16)


def widened(out, kernel_of):
    for k in range(9):
        blocks = [kernel_of(3 * k + i) for i in range(3)]
        zero = jnp.zeros_like(blocks[0])
        for j in range(4):
            row = slice(128 * (4 * k + j), 128 * (4 * k + j + 1))
            out[row, :128] = blocks[j] if j < 3 else zero
            out[row, 128:] = blocks[j - 1] if j > 0 else zero


def decoded(code, first):
    code = code[:, :27].astype(jnp.int32)
    return jnp.where(code > 0, code - 8 + first, -1024)


def tables_kernel(own, weight_hbm, gather_new, gather_back, wide, flipped, weight, sems):
    even = is_even()
    (copy,) = fetch((weight_hbm,), (weight,), sems)
    named = decoded(own[LINKS].astype(F32), lax.broadcasted_iota(jnp.int32, (16, 27), 0))
    present = named > -1024
    outside = (named < 0) | (named >= 16)
    near_side = (named >= 8) == even
    row = (named & 7) + jnp.where(named >= 16, 1, 0)
    slot = jnp.where(outside, row + jnp.where(near_side, 72, 136), named)
    slot = jnp.where(present, slot, -1024)
    for number, offsets in enumerate(MATRICES[:-1]):
        gather_new[number] = one_hot(slot, offsets, 3)
    slot = row + jnp.where(outside, 8, 0) + jnp.where(near_side, 0, 64)
    slot = jnp.where(present, slot, -1024)
    for number, offsets in enumerate(MATRICES):
        gather_back[number] = one_hot(slot, offsets, 2)
    copy.wait()
    widened(wide, lambda o: weight[o])
    widened(flipped, lambda o: weight[26 - o].T)


def fill(padded, sources, gather, count):
    for number, groups in enumerate(PLAN[:count]):
        matrix = gather(number)
        for start in range(0, len(groups), 4):
            chosen = groups[start : start + 4]
            columns = [
                jnp.concatenate([rows(u) for rows in sources for _, u in cells], axis=0) for cells in chosen
            ]
            picked = jnp.dot(
                matrix, jnp.concatenate(columns, axis=1), preferred_element_type=F32
            ).astype(BF16)
            for i, cells in enumerate(chosen):
                part = picked[:, 128 * i : 128 * i + 128].reshape(4, 16, 128)
                for j, (place, _) in enumerate(cells):
                    padded[place] = part[j]


def convolve(padded, weight, x):
    windows = []
    for dx in range(3):
        for dy in range(3):
            for j in range(4):
                windows.append(padded[x + dx : x + dx + 2, dy : dy + 4, j : j + 3 : 2].reshape(256, 128))
    both = jnp.dot(jnp.concatenate(windows, axis=1), weight[...], preferred_element_type=F32)
    halves = [both[:, 128 * h : 128 * h + 128].reshape(16, 1, 16, 128) for h in range(2)]
    return jnp.concatenate(halves, axis=1).reshape(32, 16, 128)


def sigmoid(v):
    return 1.0 / (1.0 + jnp.exp(-v))


def old_kernel(far, own, other, own_grad, wide, grad, padded):
    even = is_even()
    high = even != far
    row = lax.broadcasted_iota(jnp.int32, (8, 27), 0)
    mine = own[LINKS].astype(F32)
    theirs = other[LINKS].astype(F32)
    mine = jnp.where(high, mine[8:], mine[:8])
    theirs = jnp.where(high, pltpu.roll(theirs[:8], 1, 0), theirs[8:])
    mine = decoded(mine, jnp.where(high, row + 8, row))
    theirs = decoded(theirs, jnp.where(high, 16 + ((row + 7) & 7), row - 8))
    named = jnp.concatenate([mine, theirs], axis=0)
    slot = jnp.where((named >= 0) & (named < 16), named, (named & 15) + 64)
    slot = jnp.where(named == -1024, -1024, slot)
    tail = [tile[None, :8] for tile in read_tail(other)]
    fill(
        padded,
        (lambda u: own[u], lambda u: other[u]),
        lambda number: one_hot(slot, MATRICES[number], 2),
        COUNT,
    )
    for pair in range(2):
        v = convolve(padded, wide, 2 * pair)
        q = sigmoid(v)
        slope = q * (1.0 + v * (1.0 - q))
        part = slice(32 * pair, 32 * pair + 32)
        mine = own_grad[part].astype(F32)
        theirs = other[64 + 32 * pair : min(96 + 32 * pair, LINKS)].astype(F32)[:, :8]
        if pair == 1:
            theirs = jnp.concatenate([theirs] + tail, axis=0)
        masked = jnp.concatenate([jnp.where(high, mine[:, 8:], mine[:, :8]), theirs], axis=1)
        grad[part] = (masked * slope).astype(BF16)


def old_near_kernel(own, near, own_grad, wide, grad, padded):
    old_kernel(False, own, near.at[1 - (lax.axis_index("space") & 1)], own_grad, wide, grad, padded)


def old_far_kernel(own, far, own_grad, wide, grad, padded):
    old_kernel(True, own, far, own_grad, wide, grad, padded)


def store_bricks(out, pair, value, mask):
    part = slice(32 * pair, 32 * pair + 32)
    out[:, part] = jnp.swapaxes(value * mask[part].astype(F32), 0, 1).astype(BF16)


def new_kernel(own, near, far, mask, gather, wide, out, padded):
    near = near.at[1 - (lax.axis_index("space") & 1)]
    for x in range(4):
        for y in range(4):
            u = 16 * x + 4 * y
            padded[x + 1, y + 1, 1:5] = own[u : u + 4]
    tails = [[tile.astype(BF16) for tile in read_tail(payload)] for payload in (near, far)]

    def outer(payload, which, u):
        return payload[64 + u] if u < TAIL else tails[which][u - TAIL]

    fill(
        padded,
        (lambda u: own[u], lambda u: outer(near, 0, u), lambda u: outer(far, 1, u)),
        lambda number: gather[number],
        COUNT - 1,
    )
    for pair in range(2):
        v = convolve(padded, wide, 2 * pair)
        base = own[32 * pair : 32 * pair + 32].astype(F32)
        store_bricks(out, pair, base + v * sigmoid(v), mask)


def back_kernel(near, far, own_grad, mask, gather, flipped, out, padded):
    fill(padded, (lambda u: near[u], lambda u: far[u]), lambda number: gather[number], COUNT)
    for pair in range(2):
        v = convolve(padded, flipped, 2 * pair)
        base = own_grad[32 * pair : 32 * pair + 32].astype(F32)
        store_bricks(out, pair, base + v, mask)


PADDED = pltpu.VMEM((6, 6, 6, 16, 128), BF16)
BRICKS = pltpu.VMEM((16, 64, 128), BF16)
OCC = pltpu.VMEM((16, 64), jnp.int32)
HBM = pl.BlockSpec(memory_space=pltpu.HBM)
VMEM = pl.BlockSpec(memory_space=pltpu.VMEM)


def call(kernel, shapes, ins, out, scratch=(), flops=0):
    place = pltpu.HBM if out is HBM else pltpu.VMEM
    run = pl.pallas_call(
        kernel,
        out_shape=[place(s, BF16) for s in shapes],
        in_specs=ins,
        out_specs=[out] * len(shapes),
        scratch_shapes=list(scratch),
        compiler_params=pltpu.CompilerParams(vmem_limit_bytes=VMEM_LIMIT),
        cost_estimate=pl.CostEstimate(flops=flops, bytes_accessed=2 << 20, transcendentals=0),
    )

    def placed(*arrays):
        spaces = [pltpu.HBM if spec is HBM else pltpu.VMEM for spec in ins]
        return run(*[pltpu.with_memory_space_constraint(a, m) for a, m in zip(arrays, spaces)])

    return placed


def across(value, count):
    pairs = [(i, i + 1) for i in range(1, count - 1, 2)]
    return lax.ppermute(value, "space", pairs + [(b, a) for a, b in pairs])


def inside(value, count):
    return lax.all_gather(value, "space", axis_index_groups=[[i, i + 1] for i in range(0, count, 2)])


def flush_kernel(source, out, sem):
    copy = pltpu.make_async_copy(source, out, sem)
    copy.start()
    copy.wait()


def per_device(count, sections, incoming, saved, cotangent, occupancy, neighbours, conv_weight):
    tile = (64, 16, 128)
    payload = (LINKS + 1, 16, 128)
    send_near, send_far, own_new, own_grad, mask = call(
        prepare_kernel,
        [payload, payload, tile, tile, tile],
        [HBM] * 5,
        VMEM,
        [
            pltpu.VMEM((16, 64), jnp.int32),
            pltpu.VMEM((16, 27), jnp.int32),
            BRICKS,
            BRICKS,
            BRICKS,
            pltpu.SemaphoreType.DMA((5,)),
        ],
    )(saved[0], cotangent[0], incoming[0], occupancy[0], neighbours[0])
    far = across(send_far, count)
    gather_new, gather_back, wide, flipped = call(
        tables_kernel,
        [(COUNT - 1, 64, 192), (COUNT, 64, 128), (36 * 128, 256), (36 * 128, 256)],
        [VMEM, HBM],
        VMEM,
        [pltpu.VMEM((27, 128, 128), BF16), pltpu.SemaphoreType.DMA((1,))],
        flops=1 << 31,
    )(send_near, conv_weight[0])
    send_near, wide = lax.optimization_barrier((send_near, wide))
    near = inside(send_near, count)
    (grad_near,) = call(old_near_kernel, [tile], [VMEM] * 4, VMEM, [PADDED], flops=1 << 30)(
        send_near, near, own_grad, wide
    )
    (out,) = call(new_kernel, [(16, 64, 128)], [VMEM] * 6, VMEM, [PADDED], flops=1 << 30)(
        own_new, near, far, mask, gather_new, wide
    )
    arrived = lax.ppermute(out[None], "segment", [(s, s + 1) for s in range(sections - 1)])
    (grad_far,) = call(old_far_kernel, [tile], [VMEM] * 4, VMEM, [PADDED], flops=1 << 30)(
        send_near, far, own_grad, wide
    )
    (back,) = call(back_kernel, [(16, 64, 128)], [VMEM] * 6, VMEM, [PADDED], flops=1 << 30)(
        grad_near, grad_far, own_grad, mask, gather_back, flipped
    )
    returned = lax.ppermute(back[None], "segment", [(s + 1, s) for s in range(sections - 1)])
    (arrived,) = call(flush_kernel, [(1, 16, 64, 128)], [VMEM], HBM, [pltpu.SemaphoreType.DMA])(arrived)
    return arrived, returned


def solution(mesh):
    brick = P("segment", "space", None, None)
    index = P("segment", "space", None)
    return jax.shard_map(
        functools.partial(per_device, mesh.shape["space"], mesh.shape["segment"]),
        mesh=mesh,
        in_specs=(brick, brick, brick, index, index, P("segment", None, None, None)),
        out_specs=(brick, brick),
        check_vma=False,
    )
```

```python
import functools

import jax
import jax.numpy as jnp
from jax import lax
from jax.experimental import pallas as pl
from jax.experimental.pallas import tpu as pltpu
from jax.sharding import PartitionSpec as P

BF16 = jnp.bfloat16
F32 = jnp.float32
STEPS = (-1, 0, 1)
VMEM_LIMIT = 40 * 1024 * 1024


def source_coordinate(step, c):
    return c if step == 0 else (3 if step < 0 else 0)


def padded_coordinate(step, c):
    return c + 1 if step == 0 else (0 if step < 0 else 5)


def gather_plan():
    matrices, plan = [], []
    corners = {-1: [], 1: []}
    centre = None
    for o in range(27):
        steps = (o // 9 - 1, o // 3 % 3 - 1, o % 3 - 1)
        zeros = [a for a in range(3) if steps[a] == 0]

        def cell(c):
            source = [source_coordinate(s, v) for s, v in zip(steps, c)]
            padded = [padded_coordinate(s, v) for s, v in zip(steps, c)]
            return tuple(padded), 16 * source[0] + 4 * source[1] + source[2]

        if not zeros:
            corners[steps[1]].append((o, cell((0, 0, 0))))
            continue
        along, outer = zeros[-1], zeros[:-1]
        groups = []
        for first in range(4 ** len(outer)):
            c = [0, 0, 0]
            for a in outer:
                c[a] = first % 4
                first //= 4
            cells = []
            for second in range(4):
                c[along] = second
                cells.append(cell(c))
            groups.append(cells)
        if len(zeros) == 3:
            centre = ((o,) * 4, groups)
        else:
            matrices.append((o,) * 4)
            plan.append(groups)
    for side in (-1, 1):
        matrices.append(tuple(o for o, _ in corners[side]))
        plan.append([[c for _, c in corners[side]]])
    matrices.append(centre[0])
    plan.append(centre[1])
    return matrices, plan


MATRICES, PLAN = gather_plan()
COUNT = len(MATRICES)
TAIL = 62
LINKS = 64 + TAIL


def fetch(sources, targets, sems):
    copies = [pltpu.make_async_copy(s, t, sems.at[i]) for i, (s, t) in enumerate(zip(sources, targets))]
    for copy in copies:
        copy.start()
    return copies


def is_even():
    return (lax.axis_index("space") & 1) == 0


def voxel_major(ref, mask, block):
    part = slice(16 * block, 16 * block + 16)
    return jnp.swapaxes(ref[:, part, :].astype(F32), 0, 1) * mask[part].astype(F32)


def rows8():
    return lax.broadcasted_iota(jnp.int32, (8, 128), 0)


def stored_tail(rows, tail):
    packed = []
    for t in range(14):
        row = t % 7 + 1
        packed.append(jnp.where(rows8() == 0, pltpu.roll(tail[t // 7], 8 - row, 0), rows[t])[None])
    return jnp.concatenate(packed + [rows[14:]], axis=0)


def read_tail(payload):
    tiles = []
    for which in range(2):
        parts = [jnp.zeros((8, 128), F32)] * 2
        for row in range(1, 8):
            tile = payload[64 + 7 * which + row - 1].astype(F32)
            parts = [
                jnp.where(rows8() == row, pltpu.roll(tile[8 * h : 8 * h + 8], row, 0), parts[h]) for h in range(2)
            ]
        tiles.append(jnp.concatenate(parts, axis=0))
    return tiles


def prepare_kernel(
    saved_hbm, cotangent_hbm, incoming_hbm, occ_hbm, links_hbm,
    send_near, send_far, own_new, own_grad, mask,
    occ, links, saved, cotangent, incoming, sems,
):
    even = is_even()
    copies = fetch(
        (occ_hbm, links_hbm, saved_hbm, cotangent_hbm, incoming_hbm), (occ, links, saved, cotangent, incoming), sems
    )
    copies[0].wait()
    occupied = occ[...].astype(F32)
    for u in range(64):
        mask[u] = jnp.broadcast_to(occupied[:, u : u + 1], (16, 128)).astype(BF16)
    copies[1].wait()
    named = links[...]
    first = 16 * lax.axis_index("space") + lax.broadcasted_iota(jnp.int32, (16, 27), 0)
    code = jnp.where(named < 0, 0, named - first + 8).astype(F32)
    code = jnp.concatenate([code, jnp.zeros((16, 101), F32)], axis=1).astype(BF16)
    send_near[LINKS] = code
    send_far[LINKS] = code
    copies[2].wait()
    for block in range(4):
        part = slice(16 * block, 16 * block + 16)
        old = voxel_major(saved, mask, block).astype(BF16)
        send_near[part] = old
        send_far[part] = old
    copies[3].wait()
    copies[4].wait()
    tails = {}
    for block in (3, 1, 2, 0):
        part = slice(16 * block, 16 * block + 16)
        grad = voxel_major(cotangent, mask, block)
        new = voxel_major(incoming, mask, block)
        own_grad[part] = grad.astype(BF16)
        own_new[part] = new.astype(BF16)
        low = [pltpu.roll(v[:, :8], 1, 1) for v in (grad, new)]
        high = [v[:, 8:] for v in (grad, new)]
        for side, send in enumerate((send_near, send_far)):
            rows = [jnp.where(even == (side == 0), h, l) for h, l in zip(high, low)]
            if block == 3:
                tails[side] = [(r[14], r[15]) for r in rows]
                rows = [r[:14] for r in rows]
            if block == 0:
                rows = [stored_tail(r, tail) for r, tail in zip(rows, tails[side])]
            size = rows[0].shape[0]
            send[64 + 16 * block : 64 + 16 * block + size] = jnp.concatenate(rows, axis=1).astype(BF16)


def one_hot(slot, offsets, sources):
    shape = (64, 64 * sources)
    lane = lax.broadcasted_iota(jnp.int32, shape, 1) - 16 * (lax.broadcasted_iota(jnp.int32, shape, 0) >> 4)
    columns = jnp.concatenate([slot[:, o : o + 1] for o in offsets], axis=0)
    return jnp.where(lane == columns, 1.0, 0.0).astype(BF16)


def widened(out, kernel_of):
    for k in range(9):
        blocks = [kernel_of(3 * k + i) for i in range(3)]
        zero = jnp.zeros_like(blocks[0])
        for j in range(4):
            row = slice(128 * (4 * k + j), 128 * (4 * k + j + 1))
            out[row, :128] = blocks[j] if j < 3 else zero
            out[row, 128:] = blocks[j - 1] if j > 0 else zero


def decoded(code, first):
    code = code[:, :27].astype(jnp.int32)
    return jnp.where(code > 0, code - 8 + first, -1024)


def tables_kernel(own, weight_hbm, gather_new, gather_back, wide, flipped, weight, sems):
    even = is_even()
    (copy,) = fetch((weight_hbm,), (weight,), sems)
    named = decoded(own[LINKS].astype(F32), lax.broadcasted_iota(jnp.int32, (16, 27), 0))
    present = named > -1024
    outside = (named < 0) | (named >= 16)
    near_side = (named >= 8) == even
    row = (named & 7) + jnp.where(named >= 16, 1, 0)
    slot = jnp.where(outside, row + jnp.where(near_side, 72, 136), named)
    slot = jnp.where(present, slot, -1024)
    for number, offsets in enumerate(MATRICES[:-1]):
        gather_new[number] = one_hot(slot, offsets, 3)
    slot = row + jnp.where(outside, 8, 0) + jnp.where(near_side, 0, 64)
    slot = jnp.where(present, slot, -1024)
    for number, offsets in enumerate(MATRICES):
        gather_back[number] = one_hot(slot, offsets, 2)
    copy.wait()
    widened(wide, lambda o: weight[o])
    widened(flipped, lambda o: weight[26 - o].T)


def fill(padded, sources, gather, count):
    for number, groups in enumerate(PLAN[:count]):
        matrix = gather(number)
        for start in range(0, len(groups), 4):
            chosen = groups[start : start + 4]
            columns = [
                jnp.concatenate([rows(u) for rows in sources for _, u in cells], axis=0) for cells in chosen
            ]
            picked = jnp.dot(
                matrix, jnp.concatenate(columns, axis=1), preferred_element_type=F32
            ).astype(BF16)
            for i, cells in enumerate(chosen):
                part = picked[:, 128 * i : 128 * i + 128].reshape(4, 16, 128)
                for j, (place, _) in enumerate(cells):
                    padded[place] = part[j]


def convolve(padded, weight, x):
    windows = []
    for dx in range(3):
        for dy in range(3):
            for j in range(4):
                windows.append(padded[x + dx : x + dx + 2, dy : dy + 4, j : j + 3 : 2].reshape(256, 128))
    both = jnp.dot(jnp.concatenate(windows, axis=1), weight[...], preferred_element_type=F32)
    halves = [both[:, 128 * h : 128 * h + 128].reshape(16, 1, 16, 128) for h in range(2)]
    return jnp.concatenate(halves, axis=1).reshape(32, 16, 128)


def sigmoid(v):
    return 1.0 / (1.0 + jnp.exp(-v))


def old_kernel(far, own, other, own_grad, wide, grad, padded):
    even = is_even()
    high = even != far
    row = lax.broadcasted_iota(jnp.int32, (8, 27), 0)
    mine = own[LINKS].astype(F32)
    theirs = other[LINKS].astype(F32)
    mine = jnp.where(high, mine[8:], mine[:8])
    theirs = jnp.where(high, pltpu.roll(theirs[:8], 1, 0), theirs[8:])
    mine = decoded(mine, jnp.where(high, row + 8, row))
    theirs = decoded(theirs, jnp.where(high, 16 + ((row + 7) & 7), row - 8))
    named = jnp.concatenate([mine, theirs], axis=0)
    slot = jnp.where((named >= 0) & (named < 16), named, (named & 15) + 64)
    slot = jnp.where(named == -1024, -1024, slot)
    tail = [tile[None, :8] for tile in read_tail(other)]
    fill(
        padded,
        (lambda u: own[u], lambda u: other[u]),
        lambda number: one_hot(slot, MATRICES[number], 2),
        COUNT,
    )
    for pair in range(2):
        v = convolve(padded, wide, 2 * pair)
        q = sigmoid(v)
        slope = q * (1.0 + v * (1.0 - q))
        part = slice(32 * pair, 32 * pair + 32)
        mine = own_grad[part].astype(F32)
        theirs = other[64 + 32 * pair : min(96 + 32 * pair, LINKS)].astype(F32)[:, :8]
        if pair == 1:
            theirs = jnp.concatenate([theirs] + tail, axis=0)
        masked = jnp.concatenate([jnp.where(high, mine[:, 8:], mine[:, :8]), theirs], axis=1)
        grad[part] = (masked * slope).astype(BF16)


def old_near_kernel(own, near, own_grad, wide, grad, padded):
    old_kernel(False, own, near.at[1 - (lax.axis_index("space") & 1)], own_grad, wide, grad, padded)


def store_bricks(out, pair, value, mask):
    part = slice(32 * pair, 32 * pair + 32)
    out[:, part] = jnp.swapaxes(value * mask[part].astype(F32), 0, 1).astype(BF16)


def new_kernel(own, near, far, mask, gather, wide, out, padded):
    near = near.at[1 - (lax.axis_index("space") & 1)]
    for x in range(4):
        for y in range(4):
            u = 16 * x + 4 * y
            padded[x + 1, y + 1, 1:5] = own[u : u + 4]
    tails = [[tile.astype(BF16) for tile in read_tail(payload)] for payload in (near, far)]

    def outer(payload, which, u):
        return payload[64 + u] if u < TAIL else tails[which][u - TAIL]

    fill(
        padded,
        (lambda u: own[u], lambda u: outer(near, 0, u), lambda u: outer(far, 1, u)),
        lambda number: gather[number],
        COUNT - 1,
    )
    for pair in range(2):
        v = convolve(padded, wide, 2 * pair)
        base = own[32 * pair : 32 * pair + 32].astype(F32)
        store_bricks(out, pair, base + v * sigmoid(v), mask)


def back_kernel(near, far, own_grad, mask, gather, flipped, out, padded):
    fill(padded, (lambda u: near[u], lambda u: far[u]), lambda number: gather[number], COUNT)
    for pair in range(2):
        v = convolve(padded, flipped, 2 * pair)
        base = own_grad[32 * pair : 32 * pair + 32].astype(F32)
        store_bricks(out, pair, base + v, mask)


def finish_kernel(
    own, near, far, grad_near, own_new, own_grad, mask, gather_new, gather_back, wide, flipped,
    back, out,
    grad_far, padded_old, padded_new, padded_back,
):
    old_kernel(True, own, far, own_grad, wide, grad_far, padded_old)
    new_kernel(own_new, near, far, mask, gather_new, wide, out, padded_new)
    back_kernel(grad_near, grad_far, own_grad, mask, gather_back, flipped, back, padded_back)


PADDED = pltpu.VMEM((6, 6, 6, 16, 128), BF16)
BRICKS = pltpu.VMEM((16, 64, 128), BF16)
OCC = pltpu.VMEM((16, 64), jnp.int32)
HBM = pl.BlockSpec(memory_space=pltpu.HBM)
VMEM = pl.BlockSpec(memory_space=pltpu.VMEM)


def call(kernel, shapes, ins, out, scratch=(), flops=0):
    place = pltpu.HBM if out is HBM else pltpu.VMEM
    run = pl.pallas_call(
        kernel,
        out_shape=[place(s, BF16) for s in shapes],
        in_specs=ins,
        out_specs=[out] * len(shapes),
        scratch_shapes=list(scratch),
        compiler_params=pltpu.CompilerParams(vmem_limit_bytes=VMEM_LIMIT),
        cost_estimate=pl.CostEstimate(flops=flops, bytes_accessed=2 << 20, transcendentals=0),
    )

    def placed(*arrays):
        spaces = [pltpu.HBM if spec is HBM else pltpu.VMEM for spec in ins]
        return run(*[pltpu.with_memory_space_constraint(a, m) for a, m in zip(arrays, spaces)])

    return placed


def across(value, count):
    pairs = [(i, i + 1) for i in range(1, count - 1, 2)]
    return lax.ppermute(value, "space", pairs + [(b, a) for a, b in pairs])


def inside(value, count):
    return lax.all_gather(value, "space", axis_index_groups=[[i, i + 1] for i in range(0, count, 2)])


def flush_kernel(source, out, sem):
    copy = pltpu.make_async_copy(source, out, sem)
    copy.start()
    copy.wait()


def per_device(count, sections, incoming, saved, cotangent, occupancy, neighbours, conv_weight):
    tile = (64, 16, 128)
    payload = (LINKS + 1, 16, 128)
    send_near, send_far, own_new, own_grad, mask = call(
        prepare_kernel,
        [payload, payload, tile, tile, tile],
        [HBM] * 5,
        VMEM,
        [
            pltpu.VMEM((16, 64), jnp.int32),
            pltpu.VMEM((16, 27), jnp.int32),
            BRICKS,
            BRICKS,
            BRICKS,
            pltpu.SemaphoreType.DMA((5,)),
        ],
    )(saved[0], cotangent[0], incoming[0], occupancy[0], neighbours[0])
    far = across(send_far, count)
    gather_new, gather_back, wide, flipped = call(
        tables_kernel,
        [(COUNT - 1, 64, 192), (COUNT, 64, 128), (36 * 128, 256), (36 * 128, 256)],
        [VMEM, HBM],
        VMEM,
        [pltpu.VMEM((27, 128, 128), BF16), pltpu.SemaphoreType.DMA((1,))],
        flops=1 << 31,
    )(send_near, conv_weight[0])
    send_near, wide = lax.optimization_barrier((send_near, wide))
    near = inside(send_near, count)
    (grad_near,) = call(old_near_kernel, [tile], [VMEM] * 4, VMEM, [PADDED], flops=1 << 30)(
        send_near, near, own_grad, wide
    )
    back, out = call(
        finish_kernel,
        [(16, 64, 128)] * 2,
        [VMEM] * 11,
        VMEM,
        [pltpu.VMEM(tile, BF16), PADDED, PADDED, PADDED],
        flops=1 << 31,
    )(send_near, near, far, grad_near, own_new, own_grad, mask, gather_new, gather_back, wide, flipped)
    arrived = lax.ppermute(out[None], "segment", [(s, s + 1) for s in range(sections - 1)])
    returned = lax.ppermute(back[None], "segment", [(s + 1, s) for s in range(sections - 1)])
    (returned,) = call(flush_kernel, [(1, 16, 64, 128)], [VMEM], HBM, [pltpu.SemaphoreType.DMA])(returned)
    return arrived, returned


def solution(mesh):
    brick = P("segment", "space", None, None)
    index = P("segment", "space", None)
    return jax.shard_map(
        functools.partial(per_device, mesh.shape["space"], mesh.shape["segment"]),
        mesh=mesh,
        in_specs=(brick, brick, brick, index, index, P("segment", None, None, None)),
        out_specs=(brick, brick),
        check_vma=False,
    )
```

```python
import functools

import jax
import jax.numpy as jnp
from jax import lax
from jax.experimental import pallas as pl
from jax.experimental.pallas import tpu as pltpu
from jax.sharding import PartitionSpec as P

BF16 = jnp.bfloat16
F32 = jnp.float32
STEPS = (-1, 0, 1)
VMEM_LIMIT = 40 * 1024 * 1024


def source_coordinate(step, c):
    return c if step == 0 else (3 if step < 0 else 0)


def padded_coordinate(step, c):
    return c + 1 if step == 0 else (0 if step < 0 else 5)


def gather_plan():
    matrices, plan = [], []
    corners = {-1: [], 1: []}
    centre = None
    for o in range(27):
        steps = (o // 9 - 1, o // 3 % 3 - 1, o % 3 - 1)
        zeros = [a for a in range(3) if steps[a] == 0]

        def cell(c):
            source = [source_coordinate(s, v) for s, v in zip(steps, c)]
            padded = [padded_coordinate(s, v) for s, v in zip(steps, c)]
            return tuple(padded), 16 * source[0] + 4 * source[1] + source[2]

        if not zeros:
            corners[steps[1]].append((o, cell((0, 0, 0))))
            continue
        along, outer = zeros[-1], zeros[:-1]
        groups = []
        for first in range(4 ** len(outer)):
            c = [0, 0, 0]
            for a in outer:
                c[a] = first % 4
                first //= 4
            cells = []
            for second in range(4):
                c[along] = second
                cells.append(cell(c))
            groups.append(cells)
        if len(zeros) == 3:
            centre = ((o,) * 4, groups)
        else:
            matrices.append((o,) * 4)
            plan.append(groups)
    for side in (-1, 1):
        matrices.append(tuple(o for o, _ in corners[side]))
        plan.append([[c for _, c in corners[side]]])
    matrices.append(centre[0])
    plan.append(centre[1])
    return matrices, plan


MATRICES, PLAN = gather_plan()
COUNT = len(MATRICES)
TAIL = 62
LINKS = 64 + TAIL


def fetch(sources, targets, sems):
    copies = [pltpu.make_async_copy(s, t, sems.at[i]) for i, (s, t) in enumerate(zip(sources, targets))]
    for copy in copies:
        copy.start()
    return copies


def is_even():
    return (lax.axis_index("space") & 1) == 0


def voxel_major(ref, mask, block):
    part = slice(16 * block, 16 * block + 16)
    return jnp.swapaxes(ref[:, part, :].astype(F32), 0, 1) * mask[part].astype(F32)


def rows8():
    return lax.broadcasted_iota(jnp.int32, (8, 128), 0)


def stored_tail(rows, tail):
    packed = []
    for t in range(14):
        row = t % 7 + 1
        packed.append(jnp.where(rows8() == 0, pltpu.roll(tail[t // 7], 8 - row, 0), rows[t])[None])
    return jnp.concatenate(packed + [rows[14:]], axis=0)


def read_tail(payload):
    tiles = []
    for which in range(2):
        parts = [jnp.zeros((8, 128), F32)] * 2
        for row in range(1, 8):
            tile = payload[64 + 7 * which + row - 1].astype(F32)
            parts = [
                jnp.where(rows8() == row, pltpu.roll(tile[8 * h : 8 * h + 8], row, 0), parts[h]) for h in range(2)
            ]
        tiles.append(jnp.concatenate(parts, axis=0))
    return tiles


def prepare_kernel(
    saved_hbm, cotangent_hbm, incoming_hbm, occ_hbm, links_hbm, weight_hbm,
    send_near, send_far, own_new, own_grad, mask, weight,
    occ, links, saved, cotangent, incoming, sems,
):
    even = is_even()
    copies = fetch(
        (occ_hbm, links_hbm, saved_hbm, cotangent_hbm, incoming_hbm, weight_hbm),
        (occ, links, saved, cotangent, incoming, weight),
        sems,
    )
    copies[0].wait()
    occupied = occ[...].astype(F32)
    for u in range(64):
        mask[u] = jnp.broadcast_to(occupied[:, u : u + 1], (16, 128)).astype(BF16)
    copies[1].wait()
    named = links[...]
    first = 16 * lax.axis_index("space") + lax.broadcasted_iota(jnp.int32, (16, 27), 0)
    code = jnp.where(named < 0, 0, named - first + 8).astype(F32)
    code = jnp.concatenate([code, jnp.zeros((16, 101), F32)], axis=1).astype(BF16)
    send_near[LINKS] = code
    send_far[LINKS] = code
    copies[2].wait()
    for block in range(4):
        part = slice(16 * block, 16 * block + 16)
        old = voxel_major(saved, mask, block).astype(BF16)
        send_near[part] = old
        send_far[part] = old
    copies[3].wait()
    copies[4].wait()
    tails = {}
    for block in (3, 1, 2, 0):
        part = slice(16 * block, 16 * block + 16)
        grad = voxel_major(cotangent, mask, block)
        new = voxel_major(incoming, mask, block)
        own_grad[part] = grad.astype(BF16)
        own_new[part] = new.astype(BF16)
        low = [pltpu.roll(v[:, :8], 1, 1) for v in (grad, new)]
        high = [v[:, 8:] for v in (grad, new)]
        for side, send in enumerate((send_near, send_far)):
            rows = [jnp.where(even == (side == 0), h, l) for h, l in zip(high, low)]
            if block == 3:
                tails[side] = [(r[14], r[15]) for r in rows]
                rows = [r[:14] for r in rows]
            if block == 0:
                rows = [stored_tail(r, tail) for r, tail in zip(rows, tails[side])]
            size = rows[0].shape[0]
            send[64 + 16 * block : 64 + 16 * block + size] = jnp.concatenate(rows, axis=1).astype(BF16)
    copies[5].wait()


def one_hot(slot, offsets, sources):
    shape = (64, 64 * sources)
    lane = lax.broadcasted_iota(jnp.int32, shape, 1) - 16 * (lax.broadcasted_iota(jnp.int32, shape, 0) >> 4)
    columns = jnp.concatenate([slot[:, o : o + 1] for o in offsets], axis=0)
    return jnp.where(lane == columns, 1.0, 0.0).astype(BF16)


def widened(out, kernel_of):
    for k in range(9):
        blocks = [kernel_of(3 * k + i) for i in range(3)]
        zero = jnp.zeros_like(blocks[0])
        for j in range(4):
            row = slice(128 * (4 * k + j), 128 * (4 * k + j + 1))
            out[row, :128] = blocks[j] if j < 3 else zero
            out[row, 128:] = blocks[j - 1] if j > 0 else zero


def decoded(code, first):
    code = code[:, :27].astype(jnp.int32)
    return jnp.where(code > 0, code - 8 + first, -1024)


def tables_kernel(own, weight, gather_new, gather_back, wide, flipped):
    even = is_even()
    named = decoded(own[LINKS].astype(F32), lax.broadcasted_iota(jnp.int32, (16, 27), 0))
    present = named > -1024
    outside = (named < 0) | (named >= 16)
    near_side = (named >= 8) == even
    row = (named & 7) + jnp.where(named >= 16, 1, 0)
    slot = jnp.where(outside, row + jnp.where(near_side, 72, 136), named)
    slot = jnp.where(present, slot, -1024)
    for number, offsets in enumerate(MATRICES[:-1]):
        gather_new[number] = one_hot(slot, offsets, 3)
    slot = row + jnp.where(outside, 8, 0) + jnp.where(near_side, 0, 64)
    slot = jnp.where(present, slot, -1024)
    for number, offsets in enumerate(MATRICES):
        gather_back[number] = one_hot(slot, offsets, 2)
    widened(wide, lambda o: weight[o])
    widened(flipped, lambda o: weight[26 - o].T)


def fill(padded, sources, gather, count):
    for number, groups in enumerate(PLAN[:count]):
        matrix = gather(number)
        for start in range(0, len(groups), 4):
            chosen = groups[start : start + 4]
            columns = [
                jnp.concatenate([rows(u) for rows in sources for _, u in cells], axis=0) for cells in chosen
            ]
            picked = jnp.dot(
                matrix, jnp.concatenate(columns, axis=1), preferred_element_type=F32
            ).astype(BF16)
            for i, cells in enumerate(chosen):
                part = picked[:, 128 * i : 128 * i + 128].reshape(4, 16, 128)
                for j, (place, _) in enumerate(cells):
                    padded[place] = part[j]


def convolve(padded, weight, x):
    windows = []
    for dx in range(3):
        for dy in range(3):
            for j in range(4):
                windows.append(padded[x + dx : x + dx + 2, dy : dy + 4, j : j + 3 : 2].reshape(256, 128))
    both = jnp.dot(jnp.concatenate(windows, axis=1), weight[...], preferred_element_type=F32)
    halves = [both[:, 128 * h : 128 * h + 128].reshape(16, 1, 16, 128) for h in range(2)]
    return jnp.concatenate(halves, axis=1).reshape(32, 16, 128)


def sigmoid(v):
    return 1.0 / (1.0 + jnp.exp(-v))


def old_kernel(far, own, other, own_grad, wide, grad, padded):
    even = is_even()
    high = even != far
    row = lax.broadcasted_iota(jnp.int32, (8, 27), 0)
    mine = own[LINKS].astype(F32)
    theirs = other[LINKS].astype(F32)
    mine = jnp.where(high, mine[8:], mine[:8])
    theirs = jnp.where(high, pltpu.roll(theirs[:8], 1, 0), theirs[8:])
    mine = decoded(mine, jnp.where(high, row + 8, row))
    theirs = decoded(theirs, jnp.where(high, 16 + ((row + 7) & 7), row - 8))
    named = jnp.concatenate([mine, theirs], axis=0)
    slot = jnp.where((named >= 0) & (named < 16), named, (named & 15) + 64)
    slot = jnp.where(named == -1024, -1024, slot)
    tail = [tile[None, :8] for tile in read_tail(other)]
    fill(
        padded,
        (lambda u: own[u], lambda u: other[u]),
        lambda number: one_hot(slot, MATRICES[number], 2),
        COUNT,
    )
    for pair in range(2):
        v = convolve(padded, wide, 2 * pair)
        q = sigmoid(v)
        slope = q * (1.0 + v * (1.0 - q))
        part = slice(32 * pair, 32 * pair + 32)
        mine = own_grad[part].astype(F32)
        theirs = other[64 + 32 * pair : min(96 + 32 * pair, LINKS)].astype(F32)[:, :8]
        if pair == 1:
            theirs = jnp.concatenate([theirs] + tail, axis=0)
        masked = jnp.concatenate([jnp.where(high, mine[:, 8:], mine[:, :8]), theirs], axis=1)
        grad[part] = (masked * slope).astype(BF16)


def old_near_kernel(own, near, own_grad, wide, grad, padded):
    old_kernel(False, own, near.at[1 - (lax.axis_index("space") & 1)], own_grad, wide, grad, padded)


def store_bricks(out, pair, value, mask):
    part = slice(32 * pair, 32 * pair + 32)
    out[:, part] = jnp.swapaxes(value * mask[part].astype(F32), 0, 1).astype(BF16)


def new_kernel(own, near, far, mask, gather, wide, out, padded):
    near = near.at[1 - (lax.axis_index("space") & 1)]
    for x in range(4):
        for y in range(4):
            u = 16 * x + 4 * y
            padded[x + 1, y + 1, 1:5] = own[u : u + 4]
    tails = [[tile.astype(BF16) for tile in read_tail(payload)] for payload in (near, far)]

    def outer(payload, which, u):
        return payload[64 + u] if u < TAIL else tails[which][u - TAIL]

    fill(
        padded,
        (lambda u: own[u], lambda u: outer(near, 0, u), lambda u: outer(far, 1, u)),
        lambda number: gather[number],
        COUNT - 1,
    )
    for pair in range(2):
        v = convolve(padded, wide, 2 * pair)
        base = own[32 * pair : 32 * pair + 32].astype(F32)
        store_bricks(out, pair, base + v * sigmoid(v), mask)


def back_kernel(near, far, own_grad, mask, gather, flipped, out, padded):
    fill(padded, (lambda u: near[u], lambda u: far[u]), lambda number: gather[number], COUNT)
    for pair in range(2):
        v = convolve(padded, flipped, 2 * pair)
        base = own_grad[32 * pair : 32 * pair + 32].astype(F32)
        store_bricks(out, pair, base + v, mask)


def finish_kernel(
    own, near, far, grad_near, own_new, own_grad, mask, gather_new, gather_back, wide, flipped,
    back, out,
    grad_far, padded_old, padded_new, padded_back,
):
    old_kernel(True, own, far, own_grad, wide, grad_far, padded_old)
    new_kernel(own_new, near, far, mask, gather_new, wide, out, padded_new)
    back_kernel(grad_near, grad_far, own_grad, mask, gather_back, flipped, back, padded_back)


PADDED = pltpu.VMEM((6, 6, 6, 16, 128), BF16)
BRICKS = pltpu.VMEM((16, 64, 128), BF16)
OCC = pltpu.VMEM((16, 64), jnp.int32)
HBM = pl.BlockSpec(memory_space=pltpu.HBM)
VMEM = pl.BlockSpec(memory_space=pltpu.VMEM)


def call(kernel, shapes, ins, out, scratch=(), flops=0):
    place = pltpu.HBM if out is HBM else pltpu.VMEM
    run = pl.pallas_call(
        kernel,
        out_shape=[place(s, BF16) for s in shapes],
        in_specs=ins,
        out_specs=[out] * len(shapes),
        scratch_shapes=list(scratch),
        compiler_params=pltpu.CompilerParams(vmem_limit_bytes=VMEM_LIMIT),
        cost_estimate=pl.CostEstimate(flops=flops, bytes_accessed=2 << 20, transcendentals=0),
    )

    def placed(*arrays):
        spaces = [pltpu.HBM if spec is HBM else pltpu.VMEM for spec in ins]
        return run(*[pltpu.with_memory_space_constraint(a, m) for a, m in zip(arrays, spaces)])

    return placed


def across(value, count):
    pairs = [(i, i + 1) for i in range(1, count - 1, 2)]
    return lax.ppermute(value, "space", pairs + [(b, a) for a, b in pairs])


def inside(value, count):
    return lax.all_gather(value, "space", axis_index_groups=[[i, i + 1] for i in range(0, count, 2)])


def flush_kernel(source, out, sem):
    copy = pltpu.make_async_copy(source, out, sem)
    copy.start()
    copy.wait()


def per_device(count, sections, incoming, saved, cotangent, occupancy, neighbours, conv_weight):
    tile = (64, 16, 128)
    payload = (LINKS + 1, 16, 128)
    send_near, send_far, own_new, own_grad, mask, weight = call(
        prepare_kernel,
        [payload, payload, tile, tile, tile, (27, 128, 128)],
        [HBM] * 6,
        VMEM,
        [
            pltpu.VMEM((16, 64), jnp.int32),
            pltpu.VMEM((16, 27), jnp.int32),
            BRICKS,
            BRICKS,
            BRICKS,
            pltpu.SemaphoreType.DMA((6,)),
        ],
    )(saved[0], cotangent[0], incoming[0], occupancy[0], neighbours[0], conv_weight[0])
    far = across(send_far, count)
    gather_new, gather_back, wide, flipped = call(
        tables_kernel,
        [(COUNT - 1, 64, 192), (COUNT, 64, 128), (36 * 128, 256), (36 * 128, 256)],
        [VMEM, VMEM],
        VMEM,
        flops=1 << 31,
    )(send_near, weight)
    send_near, wide = lax.optimization_barrier((send_near, wide))
    near = inside(send_near, count)
    (grad_near,) = call(old_near_kernel, [tile], [VMEM] * 4, VMEM, [PADDED], flops=1 << 30)(
        send_near, near, own_grad, wide
    )
    back, out = call(
        finish_kernel,
        [(16, 64, 128)] * 2,
        [VMEM] * 11,
        VMEM,
        [pltpu.VMEM(tile, BF16), PADDED, PADDED, PADDED],
        flops=1 << 31,
    )(send_near, near, far, grad_near, own_new, own_grad, mask, gather_new, gather_back, wide, flipped)
    returned = lax.ppermute(back[None], "segment", [(s + 1, s) for s in range(sections - 1)])
    arrived = lax.ppermute(out[None], "segment", [(s, s + 1) for s in range(sections - 1)])
    (returned,) = call(flush_kernel, [(1, 16, 64, 128)], [VMEM], HBM, [pltpu.SemaphoreType.DMA])(returned)
    return arrived, returned


def solution(mesh):
    brick = P("segment", "space", None, None)
    index = P("segment", "space", None)
    return jax.shard_map(
        functools.partial(per_device, mesh.shape["space"], mesh.shape["segment"]),
        mesh=mesh,
        in_specs=(brick, brick, brick, index, index, P("segment", None, None, None)),
        out_specs=(brick, brick),
        check_vma=False,
    )
```

```python
import functools

import jax
import jax.numpy as jnp
from jax import lax
from jax.experimental import pallas as pl
from jax.experimental.pallas import tpu as pltpu
from jax.sharding import PartitionSpec as P

BF16 = jnp.bfloat16
F32 = jnp.float32
STEPS = (-1, 0, 1)
VMEM_LIMIT = 40 * 1024 * 1024


def source_coordinate(step, c):
    return c if step == 0 else (3 if step < 0 else 0)


def padded_coordinate(step, c):
    return c + 1 if step == 0 else (0 if step < 0 else 5)


def gather_plan():
    matrices, plan = [], []
    corners = {-1: [], 1: []}
    centre = None
    for o in range(27):
        steps = (o // 9 - 1, o // 3 % 3 - 1, o % 3 - 1)
        zeros = [a for a in range(3) if steps[a] == 0]

        def cell(c):
            source = [source_coordinate(s, v) for s, v in zip(steps, c)]
            padded = [padded_coordinate(s, v) for s, v in zip(steps, c)]
            return tuple(padded), 16 * source[0] + 4 * source[1] + source[2]

        if not zeros:
            corners[steps[1]].append((o, cell((0, 0, 0))))
            continue
        along, outer = zeros[-1], zeros[:-1]
        groups = []
        for first in range(4 ** len(outer)):
            c = [0, 0, 0]
            for a in outer:
                c[a] = first % 4
                first //= 4
            cells = []
            for second in range(4):
                c[along] = second
                cells.append(cell(c))
            groups.append(cells)
        if len(zeros) == 3:
            centre = ((o,) * 4, groups)
        else:
            matrices.append((o,) * 4)
            plan.append(groups)
    for side in (-1, 1):
        matrices.append(tuple(o for o, _ in corners[side]))
        plan.append([[c for _, c in corners[side]]])
    matrices.append(centre[0])
    plan.append(centre[1])
    return matrices, plan


MATRICES, PLAN = gather_plan()
COUNT = len(MATRICES)
TAIL = 62
LINKS = 64 + TAIL


def fetch(sources, targets, sems):
    copies = [pltpu.make_async_copy(s, t, sems.at[i]) for i, (s, t) in enumerate(zip(sources, targets))]
    for copy in copies:
        copy.start()
    return copies


def is_even():
    return (lax.axis_index("space") & 1) == 0


def voxel_major(ref, mask, block):
    part = slice(16 * block, 16 * block + 16)
    return jnp.swapaxes(ref[:, part, :].astype(F32), 0, 1) * mask[part].astype(F32)


def rows8():
    return lax.broadcasted_iota(jnp.int32, (8, 128), 0)


def stored_tail(rows, tail):
    packed = []
    for t in range(14):
        row = t % 7 + 1
        packed.append(jnp.where(rows8() == 0, pltpu.roll(tail[t // 7], 8 - row, 0), rows[t])[None])
    return jnp.concatenate(packed + [rows[14:]], axis=0)


def read_tail(payload):
    tiles = []
    for which in range(2):
        parts = [jnp.zeros((8, 128), F32)] * 2
        for row in range(1, 8):
            tile = payload[64 + 7 * which + row - 1].astype(F32)
            parts = [
                jnp.where(rows8() == row, pltpu.roll(tile[8 * h : 8 * h + 8], row, 0), parts[h]) for h in range(2)
            ]
        tiles.append(jnp.concatenate(parts, axis=0))
    return tiles


def prepare_kernel(
    saved_hbm, cotangent_hbm, incoming_hbm, occ_hbm, links_hbm, weight_hbm,
    send_near, send_far, own_new, own_grad, mask, weight,
    occ, links, saved, cotangent, incoming, sems,
):
    even = is_even()
    copies = fetch(
        (occ_hbm, links_hbm, saved_hbm, cotangent_hbm, incoming_hbm, weight_hbm),
        (occ, links, saved, cotangent, incoming, weight),
        sems,
    )
    copies[0].wait()
    occupied = occ[...].astype(F32)
    for u in range(64):
        mask[u] = jnp.broadcast_to(occupied[:, u : u + 1], (16, 128)).astype(BF16)
    copies[1].wait()
    named = links[...]
    first = 16 * lax.axis_index("space") + lax.broadcasted_iota(jnp.int32, (16, 27), 0)
    code = jnp.where(named < 0, 0, named - first + 8).astype(F32)
    code = jnp.concatenate([code, jnp.zeros((16, 101), F32)], axis=1).astype(BF16)
    send_near[LINKS] = code
    send_far[LINKS] = code
    copies[2].wait()
    for block in range(4):
        part = slice(16 * block, 16 * block + 16)
        old = voxel_major(saved, mask, block).astype(BF16)
        send_near[part] = old
        send_far[part] = old
    copies[3].wait()
    copies[4].wait()
    tails = {}
    for block in (3, 1, 2, 0):
        part = slice(16 * block, 16 * block + 16)
        grad = voxel_major(cotangent, mask, block)
        new = voxel_major(incoming, mask, block)
        own_grad[part] = grad.astype(BF16)
        own_new[part] = new.astype(BF16)
        low = [pltpu.roll(v[:, :8], 1, 1) for v in (grad, new)]
        high = [v[:, 8:] for v in (grad, new)]
        for side, send in enumerate((send_near, send_far)):
            rows = [jnp.where(even == (side == 0), h, l) for h, l in zip(high, low)]
            if block == 3:
                tails[side] = [(r[14], r[15]) for r in rows]
                rows = [r[:14] for r in rows]
            if block == 0:
                rows = [stored_tail(r, tail) for r, tail in zip(rows, tails[side])]
            size = rows[0].shape[0]
            send[64 + 16 * block : 64 + 16 * block + size] = jnp.concatenate(rows, axis=1).astype(BF16)
    copies[5].wait()


def one_hot(slot, offsets, sources):
    shape = (64, 64 * sources)
    lane = lax.broadcasted_iota(jnp.int32, shape, 1) - 16 * (lax.broadcasted_iota(jnp.int32, shape, 0) >> 4)
    columns = jnp.concatenate([slot[:, o : o + 1] for o in offsets], axis=0)
    return jnp.where(lane == columns, 1.0, 0.0).astype(BF16)


def widened(out, kernel_of):
    for k in range(9):
        blocks = [kernel_of(3 * k + i) for i in range(3)]
        zero = jnp.zeros_like(blocks[0])
        for j in range(4):
            row = slice(128 * (4 * k + j), 128 * (4 * k + j + 1))
            out[row, :128] = blocks[j] if j < 3 else zero
            out[row, 128:] = blocks[j - 1] if j > 0 else zero


def decoded(code, first):
    code = code[:, :27].astype(jnp.int32)
    return jnp.where(code > 0, code - 8 + first, -1024)


def tables_kernel(own, weight, gather_new, gather_back, wide, flipped):
    even = is_even()
    named = decoded(own[LINKS].astype(F32), lax.broadcasted_iota(jnp.int32, (16, 27), 0))
    present = named > -1024
    outside = (named < 0) | (named >= 16)
    near_side = (named >= 8) == even
    row = (named & 7) + jnp.where(named >= 16, 1, 0)
    slot = jnp.where(outside, row + jnp.where(near_side, 72, 136), named)
    slot = jnp.where(present, slot, -1024)
    for number, offsets in enumerate(MATRICES[:-1]):
        gather_new[number] = one_hot(slot, offsets, 3)
    slot = row + jnp.where(outside, 8, 0) + jnp.where(near_side, 0, 64)
    slot = jnp.where(present, slot, -1024)
    for number, offsets in enumerate(MATRICES):
        gather_back[number] = one_hot(slot, offsets, 2)
    widened(wide, lambda o: weight[o])
    widened(flipped, lambda o: weight[26 - o].T)


def fill(padded, sources, gather, count):
    for number, groups in enumerate(PLAN[:count]):
        matrix = gather(number)
        for start in range(0, len(groups), 4):
            chosen = groups[start : start + 4]
            columns = [
                jnp.concatenate([rows(u) for rows in sources for _, u in cells], axis=0) for cells in chosen
            ]
            picked = jnp.dot(
                matrix, jnp.concatenate(columns, axis=1), preferred_element_type=F32
            ).astype(BF16)
            for i, cells in enumerate(chosen):
                part = picked[:, 128 * i : 128 * i + 128].reshape(4, 16, 128)
                for j, (place, _) in enumerate(cells):
                    padded[place] = part[j]


def convolve(padded, weight, x):
    windows = []
    for dx in range(3):
        for dy in range(3):
            for j in range(4):
                windows.append(padded[x + dx : x + dx + 2, dy : dy + 4, j : j + 3 : 2].reshape(256, 128))
    both = jnp.dot(jnp.concatenate(windows, axis=1), weight[...], preferred_element_type=F32)
    halves = [both[:, 128 * h : 128 * h + 128].reshape(16, 1, 16, 128) for h in range(2)]
    return jnp.concatenate(halves, axis=1).reshape(32, 16, 128)


def sigmoid(v):
    return 0.5 * jnp.tanh(0.5 * v) + 0.5


def old_kernel(far, own, other, own_grad, wide, grad, padded):
    even = is_even()
    high = even != far
    row = lax.broadcasted_iota(jnp.int32, (8, 27), 0)
    mine = own[LINKS].astype(F32)
    theirs = other[LINKS].astype(F32)
    mine = jnp.where(high, mine[8:], mine[:8])
    theirs = jnp.where(high, pltpu.roll(theirs[:8], 1, 0), theirs[8:])
    mine = decoded(mine, jnp.where(high, row + 8, row))
    theirs = decoded(theirs, jnp.where(high, 16 + ((row + 7) & 7), row - 8))
    named = jnp.concatenate([mine, theirs], axis=0)
    slot = jnp.where((named >= 0) & (named < 16), named, (named & 15) + 64)
    slot = jnp.where(named == -1024, -1024, slot)
    tail = [tile[None, :8] for tile in read_tail(other)]
    fill(
        padded,
        (lambda u: own[u], lambda u: other[u]),
        lambda number: one_hot(slot, MATRICES[number], 2),
        COUNT,
    )
    for pair in range(2):
        v = convolve(padded, wide, 2 * pair)
        q = sigmoid(v)
        slope = q * (1.0 + v * (1.0 - q))
        part = slice(32 * pair, 32 * pair + 32)
        mine = own_grad[part].astype(F32)
        theirs = other[64 + 32 * pair : min(96 + 32 * pair, LINKS)].astype(F32)[:, :8]
        if pair == 1:
            theirs = jnp.concatenate([theirs] + tail, axis=0)
        masked = jnp.concatenate([jnp.where(high, mine[:, 8:], mine[:, :8]), theirs], axis=1)
        grad[part] = (masked * slope).astype(BF16)


def old_near_kernel(own, near, own_grad, wide, grad, padded):
    old_kernel(False, own, near.at[1 - (lax.axis_index("space") & 1)], own_grad, wide, grad, padded)


def store_bricks(out, pair, value, mask):
    part = slice(32 * pair, 32 * pair + 32)
    out[:, part] = jnp.swapaxes(value * mask[part].astype(F32), 0, 1).astype(BF16)


def new_fill(own, near, far, gather, padded):
    near = near.at[1 - (lax.axis_index("space") & 1)]
    for x in range(4):
        for y in range(4):
            u = 16 * x + 4 * y
            padded[x + 1, y + 1, 1:5] = own[u : u + 4]
    tails = [[tile.astype(BF16) for tile in read_tail(payload)] for payload in (near, far)]

    def outer(payload, which, u):
        return payload[64 + u] if u < TAIL else tails[which][u - TAIL]

    fill(
        padded,
        (lambda u: own[u], lambda u: outer(near, 0, u), lambda u: outer(far, 1, u)),
        lambda number: gather[number],
        COUNT - 1,
    )


def new_rest(own, mask, wide, out, padded):
    for pair in range(2):
        v = convolve(padded, wide, 2 * pair)
        base = own[32 * pair : 32 * pair + 32].astype(F32)
        store_bricks(out, pair, base + v * sigmoid(v), mask)


def back_kernel(near, far, own_grad, mask, gather, flipped, out, padded):
    fill(padded, (lambda u: near[u], lambda u: far[u]), lambda number: gather[number], COUNT)
    for pair in range(2):
        v = convolve(padded, flipped, 2 * pair)
        base = own_grad[32 * pair : 32 * pair + 32].astype(F32)
        store_bricks(out, pair, base + v, mask)


def finish_kernel(
    own, near, far, grad_near, own_new, own_grad, mask, gather_new, gather_back, wide, flipped,
    back, out,
    grad_far, padded_old, padded_new, padded_back,
):
    new_fill(own_new, near, far, gather_new, padded_new)
    old_kernel(True, own, far, own_grad, wide, grad_far, padded_old)
    new_rest(own_new, mask, wide, out, padded_new)
    back_kernel(grad_near, grad_far, own_grad, mask, gather_back, flipped, back, padded_back)


PADDED = pltpu.VMEM((6, 6, 6, 16, 128), BF16)
BRICKS = pltpu.VMEM((16, 64, 128), BF16)
OCC = pltpu.VMEM((16, 64), jnp.int32)
HBM = pl.BlockSpec(memory_space=pltpu.HBM)
VMEM = pl.BlockSpec(memory_space=pltpu.VMEM)


def call(kernel, shapes, ins, out, scratch=(), flops=0):
    place = pltpu.HBM if out is HBM else pltpu.VMEM
    run = pl.pallas_call(
        kernel,
        out_shape=[place(s, BF16) for s in shapes],
        in_specs=ins,
        out_specs=[out] * len(shapes),
        scratch_shapes=list(scratch),
        compiler_params=pltpu.CompilerParams(vmem_limit_bytes=VMEM_LIMIT),
        cost_estimate=pl.CostEstimate(flops=flops, bytes_accessed=2 << 20, transcendentals=0),
    )

    def placed(*arrays):
        spaces = [pltpu.HBM if spec is HBM else pltpu.VMEM for spec in ins]
        return run(*[pltpu.with_memory_space_constraint(a, m) for a, m in zip(arrays, spaces)])

    return placed


def across(value, count):
    pairs = [(i, i + 1) for i in range(1, count - 1, 2)]
    return lax.ppermute(value, "space", pairs + [(b, a) for a, b in pairs])


def inside(value, count):
    return lax.all_gather(value, "space", axis_index_groups=[[i, i + 1] for i in range(0, count, 2)])


def flush_kernel(source, out, sem):
    copy = pltpu.make_async_copy(source, out, sem)
    copy.start()
    copy.wait()


def per_device(count, sections, incoming, saved, cotangent, occupancy, neighbours, conv_weight):
    tile = (64, 16, 128)
    payload = (LINKS + 1, 16, 128)
    send_near, send_far, own_new, own_grad, mask, weight = call(
        prepare_kernel,
        [payload, payload, tile, tile, tile, (27, 128, 128)],
        [HBM] * 6,
        VMEM,
        [
            pltpu.VMEM((16, 64), jnp.int32),
            pltpu.VMEM((16, 27), jnp.int32),
            BRICKS,
            BRICKS,
            BRICKS,
            pltpu.SemaphoreType.DMA((6,)),
        ],
    )(saved[0], cotangent[0], incoming[0], occupancy[0], neighbours[0], conv_weight[0])
    far = across(send_far, count)
    gather_new, gather_back, wide, flipped = call(
        tables_kernel,
        [(COUNT - 1, 64, 192), (COUNT, 64, 128), (36 * 128, 256), (36 * 128, 256)],
        [VMEM, VMEM],
        VMEM,
        flops=1 << 31,
    )(send_near, weight)
    send_near, wide = lax.optimization_barrier((send_near, wide))
    near = inside(send_near, count)
    (grad_near,) = call(old_near_kernel, [tile], [VMEM] * 4, VMEM, [PADDED], flops=1 << 30)(
        send_near, near, own_grad, wide
    )
    back, out = call(
        finish_kernel,
        [(16, 64, 128)] * 2,
        [VMEM] * 11,
        VMEM,
        [pltpu.VMEM(tile, BF16), PADDED, PADDED, PADDED],
        flops=1 << 31,
    )(send_near, near, far, grad_near, own_new, own_grad, mask, gather_new, gather_back, wide, flipped)
    returned = lax.ppermute(back[None], "segment", [(s + 1, s) for s in range(sections - 1)])
    arrived = lax.ppermute(out[None], "segment", [(s, s + 1) for s in range(sections - 1)])
    (returned,) = call(flush_kernel, [(1, 16, 64, 128)], [VMEM], HBM, [pltpu.SemaphoreType.DMA])(returned)
    return arrived, returned


def solution(mesh):
    brick = P("segment", "space", None, None)
    index = P("segment", "space", None)
    return jax.shard_map(
        functools.partial(per_device, mesh.shape["space"], mesh.shape["segment"]),
        mesh=mesh,
        in_specs=(brick, brick, brick, index, index, P("segment", None, None, None)),
        out_specs=(brick, brick),
        check_vma=False,
    )
```

```python
import functools

import jax
import jax.numpy as jnp
from jax import lax
from jax.experimental import pallas as pl
from jax.experimental.pallas import tpu as pltpu
from jax.sharding import PartitionSpec as P

BF16 = jnp.bfloat16
F32 = jnp.float32
STEPS = (-1, 0, 1)
VMEM_LIMIT = 40 * 1024 * 1024


def source_coordinate(step, c):
    return c if step == 0 else (3 if step < 0 else 0)


def padded_coordinate(step, c):
    return c + 1 if step == 0 else (0 if step < 0 else 5)


def gather_plan():
    matrices, plan = [], []
    corners = {-1: [], 1: []}
    centre = None
    for o in range(27):
        steps = (o // 9 - 1, o // 3 % 3 - 1, o % 3 - 1)
        zeros = [a for a in range(3) if steps[a] == 0]

        def cell(c):
            source = [source_coordinate(s, v) for s, v in zip(steps, c)]
            padded = [padded_coordinate(s, v) for s, v in zip(steps, c)]
            return tuple(padded), 16 * source[0] + 4 * source[1] + source[2]

        if not zeros:
            corners[steps[1]].append((o, cell((0, 0, 0))))
            continue
        along, outer = zeros[-1], zeros[:-1]
        groups = []
        for first in range(4 ** len(outer)):
            c = [0, 0, 0]
            for a in outer:
                c[a] = first % 4
                first //= 4
            cells = []
            for second in range(4):
                c[along] = second
                cells.append(cell(c))
            groups.append(cells)
        if len(zeros) == 3:
            centre = ((o,) * 4, groups)
        else:
            matrices.append((o,) * 4)
            plan.append(groups)
    for side in (-1, 1):
        matrices.append(tuple(o for o, _ in corners[side]))
        plan.append([[c for _, c in corners[side]]])
    matrices.append(centre[0])
    plan.append(centre[1])
    return matrices, plan


MATRICES, PLAN = gather_plan()
COUNT = len(MATRICES)
TAIL = 62
LINKS = 64 + TAIL


def fetch(sources, targets, sems):
    copies = [pltpu.make_async_copy(s, t, sems.at[i]) for i, (s, t) in enumerate(zip(sources, targets))]
    for copy in copies:
        copy.start()
    return copies


def is_even():
    return (lax.axis_index("space") & 1) == 0


def voxel_major(ref, mask, block):
    part = slice(16 * block, 16 * block + 16)
    return jnp.swapaxes(ref[:, part, :].astype(F32), 0, 1) * mask[part].astype(F32)


def rows8():
    return lax.broadcasted_iota(jnp.int32, (8, 128), 0)


def stored_tail(rows, tail):
    packed = []
    for t in range(14):
        row = t % 7 + 1
        packed.append(jnp.where(rows8() == 0, pltpu.roll(tail[t // 7], 8 - row, 0), rows[t])[None])
    return jnp.concatenate(packed + [rows[14:]], axis=0)


def read_tail(payload):
    tiles = []
    for which in range(2):
        parts = [jnp.zeros((8, 128), F32)] * 2
        for row in range(1, 8):
            tile = payload[64 + 7 * which + row - 1].astype(F32)
            parts = [
                jnp.where(rows8() == row, pltpu.roll(tile[8 * h : 8 * h + 8], row, 0), parts[h]) for h in range(2)
            ]
        tiles.append(jnp.concatenate(parts, axis=0))
    return tiles


def prepare_kernel(
    saved_hbm, cotangent_hbm, incoming_hbm, occ_hbm, links_hbm, weight_hbm,
    send_near, send_far, own_new, own_grad, mask, weight,
    occ, links, saved, cotangent, incoming, sems,
):
    even = is_even()
    copies = fetch(
        (occ_hbm, links_hbm, saved_hbm, cotangent_hbm, incoming_hbm, weight_hbm),
        (occ, links, saved, cotangent, incoming, weight),
        sems,
    )
    copies[0].wait()
    occupied = occ[...].astype(F32)
    for u in range(64):
        mask[u] = jnp.broadcast_to(occupied[:, u : u + 1], (16, 128)).astype(BF16)
    copies[1].wait()
    named = links[...]
    first = 16 * lax.axis_index("space") + lax.broadcasted_iota(jnp.int32, (16, 27), 0)
    code = jnp.where(named < 0, 0, named - first + 8).astype(F32)
    code = jnp.concatenate([code, jnp.zeros((16, 101), F32)], axis=1).astype(BF16)
    send_near[LINKS] = code
    send_far[LINKS] = code
    copies[2].wait()
    for block in range(4):
        part = slice(16 * block, 16 * block + 16)
        old = voxel_major(saved, mask, block).astype(BF16)
        send_near[part] = old
        send_far[part] = old
    copies[3].wait()
    copies[4].wait()
    tails = {}
    for block in (3, 1, 2, 0):
        part = slice(16 * block, 16 * block + 16)
        grad = voxel_major(cotangent, mask, block)
        new = voxel_major(incoming, mask, block)
        own_grad[part] = grad.astype(BF16)
        own_new[part] = new.astype(BF16)
        low = [pltpu.roll(v[:, :8], 1, 1) for v in (grad, new)]
        high = [v[:, 8:] for v in (grad, new)]
        for side, send in enumerate((send_near, send_far)):
            rows = [jnp.where(even == (side == 0), h, l) for h, l in zip(high, low)]
            if block == 3:
                tails[side] = [(r[14], r[15]) for r in rows]
                rows = [r[:14] for r in rows]
            if block == 0:
                rows = [stored_tail(r, tail) for r, tail in zip(rows, tails[side])]
            size = rows[0].shape[0]
            send[64 + 16 * block : 64 + 16 * block + size] = jnp.concatenate(rows, axis=1).astype(BF16)
    copies[5].wait()


def one_hot(slot, offsets, sources):
    shape = (64, 64 * sources)
    lane = lax.broadcasted_iota(jnp.int32, shape, 1) - 16 * (lax.broadcasted_iota(jnp.int32, shape, 0) >> 4)
    columns = jnp.concatenate([slot[:, o : o + 1] for o in offsets], axis=0)
    return jnp.where(lane == columns, 1.0, 0.0).astype(BF16)


def widened(out, kernel_of):
    for k in range(9):
        blocks = [kernel_of(3 * k + i) for i in range(3)]
        zero = jnp.zeros_like(blocks[0])
        for j in range(4):
            row = slice(128 * (4 * k + j), 128 * (4 * k + j + 1))
            out[row, :128] = blocks[j] if j < 3 else zero
            out[row, 128:] = blocks[j - 1] if j > 0 else zero


def decoded(code, first):
    code = code[:, :27].astype(jnp.int32)
    return jnp.where(code > 0, code - 8 + first, -1024)


def tables_kernel(own, weight, gather_new, gather_back, wide, flipped):
    even = is_even()
    named = decoded(own[LINKS].astype(F32), lax.broadcasted_iota(jnp.int32, (16, 27), 0))
    present = named > -1024
    outside = (named < 0) | (named >= 16)
    near_side = (named >= 8) == even
    row = (named & 7) + jnp.where(named >= 16, 1, 0)
    slot = jnp.where(outside, row + jnp.where(near_side, 72, 136), named)
    slot = jnp.where(present, slot, -1024)
    for number, offsets in enumerate(MATRICES[:-1]):
        gather_new[number] = one_hot(slot, offsets, 3)
    slot = row + jnp.where(outside, 8, 0) + jnp.where(near_side, 0, 64)
    slot = jnp.where(present, slot, -1024)
    for number, offsets in enumerate(MATRICES):
        gather_back[number] = one_hot(slot, offsets, 2)
    widened(wide, lambda o: weight[o])
    widened(flipped, lambda o: weight[26 - o].T)


def fill(padded, sources, gather, count):
    for number, groups in enumerate(PLAN[:count]):
        matrix = gather(number)
        for start in range(0, len(groups), 4):
            chosen = groups[start : start + 4]
            columns = [
                jnp.concatenate([rows(u) for rows in sources for _, u in cells], axis=0) for cells in chosen
            ]
            picked = jnp.dot(
                matrix, jnp.concatenate(columns, axis=1), preferred_element_type=F32
            ).astype(BF16)
            for i, cells in enumerate(chosen):
                part = picked[:, 128 * i : 128 * i + 128].reshape(4, 16, 128)
                for j, (place, _) in enumerate(cells):
                    padded[place] = part[j]


def convolve(padded, weight, x):
    windows = []
    for dx in range(3):
        for dy in range(3):
            for j in range(4):
                windows.append(padded[x + dx : x + dx + 2, dy : dy + 4, j : j + 3 : 2].reshape(256, 128))
    both = jnp.dot(jnp.concatenate(windows, axis=1), weight[...], preferred_element_type=F32)
    halves = [both[:, 128 * h : 128 * h + 128].reshape(16, 1, 16, 128) for h in range(2)]
    return jnp.concatenate(halves, axis=1).reshape(32, 16, 128)


def sigmoid(v):
    return 1.0 / (1.0 + jnp.exp(-v))


def old_kernel(far, own, other, own_grad, wide, grad, padded):
    even = is_even()
    high = even != far
    row = lax.broadcasted_iota(jnp.int32, (8, 27), 0)
    mine = own[LINKS].astype(F32)
    theirs = other[LINKS].astype(F32)
    mine = jnp.where(high, mine[8:], mine[:8])
    theirs = jnp.where(high, pltpu.roll(theirs[:8], 1, 0), theirs[8:])
    mine = decoded(mine, jnp.where(high, row + 8, row))
    theirs = decoded(theirs, jnp.where(high, 16 + ((row + 7) & 7), row - 8))
    named = jnp.concatenate([mine, theirs], axis=0)
    slot = jnp.where((named >= 0) & (named < 16), named, (named & 15) + 64)
    slot = jnp.where(named == -1024, -1024, slot)
    tail = [tile[None, :8] for tile in read_tail(other)]
    fill(
        padded,
        (lambda u: own[u], lambda u: other[u]),
        lambda number: one_hot(slot, MATRICES[number], 2),
        COUNT,
    )
    for pair in range(2):
        v = convolve(padded, wide, 2 * pair)
        q = sigmoid(v)
        slope = q * (1.0 + v * (1.0 - q))
        part = slice(32 * pair, 32 * pair + 32)
        mine = own_grad[part].astype(F32)
        theirs = other[64 + 32 * pair : min(96 + 32 * pair, LINKS)].astype(F32)[:, :8]
        if pair == 1:
            theirs = jnp.concatenate([theirs] + tail, axis=0)
        masked = jnp.concatenate([jnp.where(high, mine[:, 8:], mine[:, :8]), theirs], axis=1)
        grad[part] = (masked * slope).astype(BF16)


def old_near_kernel(own, near, own_grad, wide, grad, padded):
    old_kernel(False, own, near.at[1 - (lax.axis_index("space") & 1)], own_grad, wide, grad, padded)


def store_bricks(out, pair, value, mask):
    part = slice(32 * pair, 32 * pair + 32)
    out[:, part] = jnp.swapaxes(value * mask[part].astype(F32), 0, 1).astype(BF16)


def new_kernel(own, near, far, mask, gather, wide, out, padded):
    near = near.at[1 - (lax.axis_index("space") & 1)]
    for x in range(4):
        for y in range(4):
            u = 16 * x + 4 * y
            padded[x + 1, y + 1, 1:5] = own[u : u + 4]
    tails = [[tile.astype(BF16) for tile in read_tail(payload)] for payload in (near, far)]

    def outer(payload, which, u):
        return payload[64 + u] if u < TAIL else tails[which][u - TAIL]

    fill(
        padded,
        (lambda u: own[u], lambda u: outer(near, 0, u), lambda u: outer(far, 1, u)),
        lambda number: gather[number],
        COUNT - 1,
    )
    for pair in range(2):
        v = convolve(padded, wide, 2 * pair)
        base = own[32 * pair : 32 * pair + 32].astype(F32)
        store_bricks(out, pair, base + v * sigmoid(v), mask)


def back_kernel(near, far, own_grad, mask, gather, flipped, out, padded):
    fill(padded, (lambda u: near[u], lambda u: far[u]), lambda number: gather[number], COUNT)
    for pair in range(2):
        v = convolve(padded, flipped, 2 * pair)
        base = own_grad[32 * pair : 32 * pair + 32].astype(F32)
        store_bricks(out, pair, base + v, mask)


def finish_kernel(
    own, near, far, grad_near, own_new, own_grad, mask, gather_new, gather_back, wide, flipped,
    back, out,
    grad_far, padded_old, padded_new, padded_back,
):
    old_kernel(True, own, far, own_grad, wide, grad_far, padded_old)
    new_kernel(own_new, near, far, mask, gather_new, wide, out, padded_new)
    back_kernel(grad_near, grad_far, own_grad, mask, gather_back, flipped, back, padded_back)


PADDED = pltpu.VMEM((6, 6, 6, 16, 128), BF16)
BRICKS = pltpu.VMEM((16, 64, 128), BF16)
OCC = pltpu.VMEM((16, 64), jnp.int32)
HBM = pl.BlockSpec(memory_space=pltpu.HBM)
VMEM = pl.BlockSpec(memory_space=pltpu.VMEM)


def call(kernel, shapes, ins, out, scratch=(), flops=0):
    place = pltpu.HBM if out is HBM else pltpu.VMEM
    run = pl.pallas_call(
        kernel,
        out_shape=[place(s, BF16) for s in shapes],
        in_specs=ins,
        out_specs=[out] * len(shapes),
        scratch_shapes=list(scratch),
        compiler_params=pltpu.CompilerParams(vmem_limit_bytes=VMEM_LIMIT),
        cost_estimate=pl.CostEstimate(flops=flops, bytes_accessed=2 << 20, transcendentals=0),
    )

    def placed(*arrays):
        spaces = [pltpu.HBM if spec is HBM else pltpu.VMEM for spec in ins]
        return run(*[pltpu.with_memory_space_constraint(a, m) for a, m in zip(arrays, spaces)])

    return placed


def across(value, count):
    pairs = [(i, i + 1) for i in range(1, count - 1, 2)]
    return lax.ppermute(value, "space", pairs + [(b, a) for a, b in pairs])


def inside(value, count):
    return lax.all_gather(value, "space", axis_index_groups=[[i, i + 1] for i in range(0, count, 2)])


def flush_kernel(first, second, first_out, second_out, sems):
    for copy in fetch((first, second), (first_out, second_out), sems):
        copy.wait()


def per_device(count, sections, incoming, saved, cotangent, occupancy, neighbours, conv_weight):
    tile = (64, 16, 128)
    payload = (LINKS + 1, 16, 128)
    send_near, send_far, own_new, own_grad, mask, weight = call(
        prepare_kernel,
        [payload, payload, tile, tile, tile, (27, 128, 128)],
        [HBM] * 6,
        VMEM,
        [
            pltpu.VMEM((16, 64), jnp.int32),
            pltpu.VMEM((16, 27), jnp.int32),
            BRICKS,
            BRICKS,
            BRICKS,
            pltpu.SemaphoreType.DMA((6,)),
        ],
    )(saved[0], cotangent[0], incoming[0], occupancy[0], neighbours[0], conv_weight[0])
    far = across(send_far, count)
    gather_new, gather_back, wide, flipped = call(
        tables_kernel,
        [(COUNT - 1, 64, 192), (COUNT, 64, 128), (36 * 128, 256), (36 * 128, 256)],
        [VMEM, VMEM],
        VMEM,
        flops=1 << 31,
    )(send_near, weight)
    send_near, wide = lax.optimization_barrier((send_near, wide))
    near = inside(send_near, count)
    (grad_near,) = call(old_near_kernel, [tile], [VMEM] * 4, VMEM, [PADDED], flops=1 << 30)(
        send_near, near, own_grad, wide
    )
    back, out = call(
        finish_kernel,
        [(16, 64, 128)] * 2,
        [VMEM] * 11,
        VMEM,
        [pltpu.VMEM(tile, BF16), PADDED, PADDED, PADDED],
        flops=1 << 31,
    )(send_near, near, far, grad_near, own_new, own_grad, mask, gather_new, gather_back, wide, flipped)
    returned = lax.ppermute(back[None], "segment", [(s + 1, s) for s in range(sections - 1)])
    arrived = lax.ppermute(out[None], "segment", [(s, s + 1) for s in range(sections - 1)])
    arrived, returned = call(
        flush_kernel, [(1, 16, 64, 128)] * 2, [VMEM] * 2, HBM, [pltpu.SemaphoreType.DMA((2,))]
    )(arrived, returned)
    return arrived, returned


def solution(mesh):
    brick = P("segment", "space", None, None)
    index = P("segment", "space", None)
    return jax.shard_map(
        functools.partial(per_device, mesh.shape["space"], mesh.shape["segment"]),
        mesh=mesh,
        in_specs=(brick, brick, brick, index, index, P("segment", None, None, None)),
        out_specs=(brick, brick),
        check_vma=False,
    )
```
